32 devices in a mesh: dp: 8 (over z, core), head: 4 (over y, x).
Axes of the slice: x: 2, y: 2, z: 4, core: 2. Of those that a mesh axis runs over, the one named last changes fastest.
Arguments:
- tokens: bfloat16 [4, 4096, 2048], P(None, ('dp', 'head')), may hold values from -6 to 6
- cotangent: bfloat16 [4, 4096, 2048], P(None, ('dp', 'head')), may hold values from -6 to 6
- token_counts: int32 [4, 8], P(None, 'dp'), may hold values from 1 to 512, 3072 in all within a row
- doc_lengths: int32 [4, 8, 4], P(None, 'dp'), may hold values from 1 to 256, 512 in all within a row
- norm_in: float32 [2048], replicated, may hold values from 0.5 to 1.5
- w_query: bfloat16 [2048, 2048], P(None, 'head'), may hold values from -0.125 to 0.125
- w_key: bfloat16 [2048, 2048], P(None, 'head'), may hold values from -0.125 to 0.125
- w_value: bfloat16 [2048, 2048], P(None, 'head'), may hold values from -0.125 to 0.125
- w_outgate: bfloat16 [2048, 2048], P(None, 'head'), may hold values from -0.125 to 0.125
- w_decay: bfloat16 [2048, 16], P(None, 'head'), may hold values from -0.125 to 0.125
- w_beta: bfloat16 [2048, 16], P(None, 'head'), may hold values from -0.125 to 0.125
- conv_weight: float32 [3, 4, 2048], P(None, None, 'head'), may hold values from -3 to 3
- decay_log: float32 [16], P('head'), may hold values from -6.9 to -3
- dt_bias: float32 [16], P('head'), may hold values from -1 to 1
- gain_out: float32 [2048], P('head'), may hold values from 0.5 to 1.5
- w_out: bfloat16 [2048, 2048], P('head'), may hold values from -0.25 to 0.25
- norm_mid: float32 [2048], replicated, may hold values from 0.5 to 1.5
- w_gate: bfloat16 [2048, 5632], P('dp', 'head'), may hold values from -0.125 to 0.125
- w_up: bfloat16 [2048, 5632], P('dp', 'head'), may hold values from -0.125 to 0.125
- w_down: bfloat16 [2048, 5632], P('dp', 'head'), may hold values from -0.15625 to 0.15625
Outputs:
- block_out: bfloat16 [4, 4096, 2048], P(None, ('dp', 'head'))
- grad_tokens: bfloat16 [4, 4096, 2048], P(None, ('dp', 'head'))
- grad_norm_in: float32 [2048], replicated
- grad_query: float32 [2048, 2048], P('dp', 'head')
- grad_key: float32 [2048, 2048], P('dp', 'head')
- grad_value: float32 [2048, 2048], P('dp', 'head')
- grad_outgate: float32 [2048, 2048], P('dp', 'head')
- grad_decay: float32 [2048, 16], P('dp', 'head')
- grad_beta: float32 [2048, 16], P('dp', 'head')
- grad_conv: float32 [3, 4, 2048], P(None, None, 'head')
- grad_decay_log: float32 [16], P('head')
- grad_dt_bias: float32 [16], P('head')
- grad_gain_out: float32 [2048], P('head')
- grad_out_proj: float32 [2048, 2048], P('head', 'dp')
- grad_norm_mid: float32 [2048], replicated
- grad_gate: float32 [2048, 5632], P('dp', 'head')
- grad_up: float32 [2048, 5632], P('dp', 'head')
- grad_down: float32 [2048, 5632], P('dp', 'head')
The draws below stay inside these ranges and needn't reach their ends.
Inputs may be any that keep to these rules, and one draw needn't show every extreme that they name: `token_counts`: the counts of one micro-batch sum to three quarters of its 4096 slots, and one of them equals 512; slots from the count on are padding whose cotangent is dropped. `doc_lengths`: each buffer's lengths fill its 512 slots; one length of each buffer equals half of 512.
All inputs are finite; a program needn't handle non-finite values. No bound on the sum of `token_counts` on one device may be relied on, other than what follows from the above.
Results may differ from the reference program's by a relative error of at most 0.019.
Values may be sent and summed in bfloat16 or wider, within the bound.
A program may use at most 640 MiB of HBM per device.

```python
import math
import jax
import jax.numpy as jnp
import numpy as np
from jax import lax

D = 2048
H = 16
HD = 128
FF = 5632
CONV = 4
GROUP = 64
MICRO = 4
DOCS = 4
SEQ = 512
TOKENS = 4096
N_DP = 8


def levels(key, extent, cuts, smallest, top_value):
    factor_of, own = 1.0, jax.random.fold_in(key, 6)
    for dim, shards_of in cuts:
        steps = jnp.exp(jax.random.uniform(jax.random.fold_in(own, dim), (shards_of,), jnp.float32, smallest / len(cuts), top_value / len(cuts)))
        factor_of = factor_of * jnp.repeat(steps, extent[dim] // shards_of).reshape([-1 if axis == dim else 1 for axis in range(len(extent))])
    return factor_of


def length_profile(amount, total, bound, skew):
    loads = [(1 << 20) // math.isqrt(rank ** skew) + 1 for rank in range(2, amount + 1)]
    rest, counts = total - bound - (amount - 1), [1] * (amount - 1)
    while rest > 0:
        candidates = [i for i in range(amount - 1) if counts[i] < bound]
        whole, budget = sum([loads[i] for i in candidates]), rest
        for i in candidates:
            addition = min(bound - counts[i], max(1, budget * loads[i] // whole), rest)
            counts[i] = counts[i] + addition
            rest = rest - addition
    return np.array([bound] + counts)


def uneven_parts(key, count, total, limit, skew):
    if count == 2:
        one = jax.random.randint(key, (), max(1, total - limit), min(limit, total - 1) + 1)
        return jnp.stack([one, total - one])
    sizes = jnp.asarray(length_profile(count, total, limit, skew), jnp.int32)
    couples = (count - 1) // 2
    donor, taker = sizes[1:1 + 2 * couples:2], sizes[2:2 + 2 * couples:2]
    slack = jnp.minimum(donor - 1, limit - taker)
    shifted = jax.random.randint(jax.random.fold_in(key, 1), (couples,), 0, 1 << 20) % (slack + 1)
    sizes = sizes.at[1:1 + 2 * couples:2].set(donor - shifted).at[2:2 + 2 * couples:2].set(taker + shifted)
    return sizes[jax.random.permutation(jax.random.fold_in(key, 2), count)]


def scatter_about(stream_key, shape, spread, limit, split=(), kind=jnp.bfloat16):
    drawn = jax.random.normal(stream_key, shape, jnp.float32) * spread
    if len(split) > 0:
        drawn = levels(stream_key, shape, split, -0.22, 0.18) * drawn
    return jnp.clip(drawn, min=-limit, max=limit).astype(kind)


def setup_inputs(seed: int = 0) -> dict:
    key_list = jax.random.split(jax.random.key(seed), 21)
    return {
        "tokens": scatter_about(key_list[0], (MICRO, TOKENS, D), 1.0, 6.0, ((1, 32),)),
        "cotangent": scatter_about(key_list[1], (MICRO, TOKENS, D), 1.0, 6.0, ((1, 32),)),
        "token_counts": jax.vmap(lambda own: uneven_parts(own, N_DP, N_DP * SEQ * 3 // 4, SEQ, 1))(jax.random.split(key_list[2], MICRO)).reshape((MICRO, N_DP)).astype(jnp.int32),
        "doc_lengths": jax.vmap(lambda own: uneven_parts(own, DOCS, SEQ, SEQ // 2, 1))(jax.random.split(key_list[3], MICRO * N_DP)).reshape((MICRO, N_DP, DOCS)).astype(jnp.int32),
        "norm_in": jnp.clip(1.0 + 0.1 * jax.random.normal(key_list[4], (D,), jnp.float32), 0.5, 1.5),
        "w_query": scatter_about(key_list[5], (D, D), D ** -0.5, 0.125, ((1, 4),)),
        "w_key": scatter_about(key_list[6], (D, D), D ** -0.5, 0.125, ((1, 4),)),
        "w_value": scatter_about(key_list[7], (D, D), D ** -0.5, 0.125, ((1, 4),)),
        "w_outgate": scatter_about(key_list[8], (D, D), D ** -0.5, 0.125, ((1, 4),)),
        "w_decay": scatter_about(key_list[9], (D, H), D ** -0.5, 0.125, ((1, 4),)),
        "w_beta": scatter_about(key_list[10], (D, H), D ** -0.5, 0.125, ((1, 4),)),
        "conv_weight": scatter_about(key_list[11], (3, CONV, D), 0.5, 3.0, ((2, 4),), jnp.float32),
        "decay_log": jnp.clip(-6.9 + 3.9 * jax.random.uniform(key_list[12], (H,), jnp.float32) ** levels(key_list[12], (H,), ((0, 4),), -0.2, 0.2), -6.9, -3.0),
        "dt_bias": jnp.clip(jax.random.uniform(key_list[13], (H,), jnp.float32, -1.0, 1.0) * levels(key_list[13], (H,), ((0, 4),), -0.4, 0.0), -1.0, 1.0),
        "gain_out": jnp.clip(1.0 + 0.1 * jax.random.normal(key_list[14], (D,), jnp.float32), 0.5, 1.5),
        "w_out": scatter_about(key_list[15], (D, D), (D // 4) ** -0.5, 0.25, ((0, 4),)),
        "norm_mid": jnp.clip(1.0 + 0.1 * jax.random.normal(key_list[16], (D,), jnp.float32), 0.5, 1.5),
        "w_gate": scatter_about(key_list[17], (D, FF), D ** -0.5, 0.125, ((0, 8), (1, 4))),
        "w_up": scatter_about(key_list[18], (D, FF), D ** -0.5, 0.125, ((0, 8), (1, 4))),
        "w_down": scatter_about(key_list[19], (D, FF), (FF // 4) ** -0.5, 0.15625, ((0, 8), (1, 4))),
    }


HIGH = lax.Precision.HIGHEST

@jax.custom_vjp
def low(v):
    return lax.optimization_barrier(v.astype(jnp.bfloat16)).astype(jnp.float32)

@jax.custom_vjp
def low_back(v):
    return v

def low_keep(v):
    return (low(v), None)

def low_pass(kept, grad):
    return (grad,)

def back_keep(v):
    return (v, None)

def back_low(kept, grad):
    return (low(grad),)
low.defvjp(low_keep, low_pass)
low_back.defvjp(back_keep, back_low)

def product(left, right):
    return jnp.dot(left, right, precision=HIGH)

def norm_rows(values, gain):
    return values * lax.rsqrt(lax.optimization_barrier(jnp.mean(values * values, axis=-1, keepdims=True)) + 1e-05) * gain

def unit_rows(values):
    return values * lax.rsqrt(lax.optimization_barrier(jnp.sum(values * values, axis=-1, keepdims=True)) + 1e-06)

def causal_conv(values, weight, segment):
    summed = values * weight[0]
    for offset in range(1, CONV):
        earlier = jnp.pad(values, ((0, 0), (offset, 0), (0, 0)))[:, :-offset]
        earlier_segment = jnp.pad(segment, ((0, 0), (offset, 0)), constant_values=-1)[:, :-offset]
        summed = summed + earlier * weight[offset] * (earlier_segment == segment)[:, :, None].astype(jnp.float32)
    return summed

def delta_rule(query, key_vec, value, log_alpha, beta, fresh):
    batch = query.shape[0]
    heads = query.shape[2]

    def to_blocks(values):
        moved = jnp.moveaxis(values, 1, 0)
        return moved.reshape((SEQ // GROUP, GROUP) + moved.shape[1:])

    def token_step(state, inputs):
        query_t, key_t, value_t, log_t, beta_t, fresh_t = inputs
        state = state * (1.0 - fresh_t)[:, None, None, None]
        alpha = jnp.exp(log_t)[:, :, None]
        recalled = jnp.einsum('bhvk,bhk->bhv', state, key_t, precision=HIGH)
        change = beta_t[:, :, None] * (value_t - alpha * recalled)
        state = alpha[:, :, :, None] * state + change[:, :, :, None] * key_t[:, :, None, :]
        return (state, jnp.einsum('bhvk,bhk->bhv', state, query_t, precision=HIGH))

    @jax.checkpoint
    def block_step(state, block):
        return lax.scan(token_step, state, block)
    initial = jnp.zeros((batch, heads, HD, HD), jnp.float32)
    blocks = tuple((to_blocks(item) for item in (query, key_vec, value, log_alpha, beta, fresh)))
    final, outputs = lax.scan(block_step, initial, blocks)
    outputs = outputs.reshape((SEQ, batch, heads, HD))
    return jnp.moveaxis(outputs, 0, 1)

def forward(params, inputs, segment):
    norm_in, w_query, w_key, w_value, w_outgate, w_decay, w_beta, conv_weight, decay_log, dt_bias, gain_out, w_out, norm_mid, w_gate, w_up, w_down = params
    batch = inputs.shape[0]
    flat = inputs.reshape(-1, D)
    normed = low(norm_rows(flat, norm_in))
    query_raw = low_back(product(normed, w_query))
    key_raw = low_back(product(normed, w_key))
    value_raw = low_back(product(normed, w_value))
    outgate_raw = low_back(product(normed, w_outgate))
    decay_raw = low_back(product(normed, w_decay))
    beta_raw = low_back(product(normed, w_beta))

    def by_buffer(values):
        return values.reshape(batch, SEQ, -1)
    query = jax.nn.silu(causal_conv(by_buffer(query_raw), conv_weight[0], segment))
    key_vec = jax.nn.silu(causal_conv(by_buffer(key_raw), conv_weight[1], segment))
    value = jax.nn.silu(causal_conv(by_buffer(value_raw), conv_weight[2], segment))
    query = unit_rows(query.reshape(batch, SEQ, H, HD)) * HD ** (-0.5)
    key_vec = unit_rows(key_vec.reshape(batch, SEQ, H, HD))
    value = value.reshape(batch, SEQ, H, HD)
    log_alpha = -jnp.exp(decay_log) * jax.nn.softplus(by_buffer(decay_raw) + dt_bias)
    beta = jax.nn.sigmoid(by_buffer(beta_raw))
    prior = jnp.pad(segment, ((0, 0), (1, 0)), constant_values=-1)[:, :-1]
    fresh = (segment != prior).astype(jnp.float32)
    core = delta_rule(query, key_vec, value, log_alpha, beta, fresh)
    core = core * lax.rsqrt(lax.optimization_barrier(jnp.mean(core * core, axis=-1, keepdims=True)) + 1e-05)
    mixed = low(core.reshape(-1, D) * gain_out * jax.nn.silu(outgate_raw))
    attn = low_back(product(mixed, w_out))
    resid = flat + attn
    normed_mid = low(norm_rows(resid, norm_mid))
    gate = low_back(product(normed_mid, w_gate))
    up = low_back(product(normed_mid, w_up))
    act = low(jax.nn.silu(gate) * up)
    ffn = low_back(product(act, w_down.T))
    return (resid + ffn).reshape(inputs.shape)

def reference(tokens, cotangent, token_counts, doc_lengths, norm_in, w_query, w_key, w_value, w_outgate, w_decay, w_beta, conv_weight, decay_log, dt_bias, gain_out, w_out, norm_mid, w_gate, w_up, w_down):
    params = tuple((item.astype(jnp.float32) for item in (norm_in, w_query, w_key, w_value, w_outgate, w_decay, w_beta, conv_weight, decay_log, dt_bias, gain_out, w_out, norm_mid, w_gate, w_up, w_down)))
    inputs_all = tokens.astype(jnp.float32).reshape(MICRO, N_DP, SEQ, D)
    places = jnp.arange(SEQ, dtype=jnp.int32)
    live = (places[None, None, :] < token_counts[:, :, None]).astype(jnp.float32)
    grads_all = cotangent.astype(jnp.float32).reshape(MICRO, N_DP, SEQ, D) * live[:, :, :, None]
    ends = jnp.cumsum(doc_lengths, axis=-1)
    segments = lax.optimization_barrier(jnp.sum((places[None, None, :, None] >= ends[:, :, None, :]).astype(jnp.int32), axis=-1)).astype(jnp.int32)

    def micro_step(totals, item):
        inputs, grad_out, segment = item
        result, pull = jax.vjp(lambda weights, values: forward(weights, values, segment), params, inputs)
        weight_grads, input_grad = pull(grad_out)
        totals = jax.tree.map(lambda left, right: left + right, totals, weight_grads)
        return (totals, (result.astype(jnp.bfloat16), input_grad.astype(jnp.bfloat16)))
    zeros = jax.tree.map(jnp.zeros_like, params)
    totals, (results, input_grads) = lax.scan(micro_step, zeros, (inputs_all, grads_all, segments))
    results = results.reshape(MICRO, TOKENS, D)
    input_grads = input_grads.reshape(MICRO, TOKENS, D)
    return (results, input_grads, totals[0], totals[1], totals[2], totals[3], totals[4], totals[5], totals[6], totals[7], totals[8], totals[9], totals[10], totals[11], totals[12], totals[13], totals[14], totals[15])
```

```python
import jax
import jax.numpy as jnp
from jax import lax
from jax.experimental import pallas as pl
from jax.experimental.pallas import tpu as pltpu
from jax.sharding import PartitionSpec as P

HD = 128
LANES = 128
SCALE = HD ** (-0.5)
BF = jnp.bfloat16
F32 = jnp.float32


def norm_rows(values, gain):
    return values * lax.rsqrt(jnp.mean(values * values, axis=-1, keepdims=True) + 1e-05) * gain


def swiglu(gate, upward):
    return jax.nn.silu(gate) * upward


def mm(left, right):
    return jnp.dot(left.astype(BF), right.astype(BF), preferred_element_type=F32)


def mm_nt(left, right):
    return lax.dot_general(
        left.astype(BF), right.astype(BF), (((1,), (1,)), ((), ())), preferred_element_type=F32
    )


def mm_tn(left, right):
    return lax.dot_general(
        left.astype(BF), right.astype(BF), (((0,), (0,)), ((), ())), preferred_element_type=F32
    )


def mm_exact(left, right):
    return jnp.dot(left, right, preferred_element_type=F32, precision=lax.Precision.HIGHEST)


def sigmoid(values):
    return 1.0 / (1.0 + jnp.exp(-values))


def softplus(values):
    return jnp.maximum(values, 0.0) + jnp.log(1.0 + jnp.exp(-jnp.abs(values)))


def chunk_gates(small, scal_ref, aux, heads):
    rows = small.shape[0]
    row_ids = lax.broadcasted_iota(jnp.int32, (rows, rows), 0)
    col_ids = lax.broadcasted_iota(jnp.int32, (rows, rows), 1)
    log_alpha = scal_ref[0:1, :] * softplus(small + scal_ref[1:2, :])
    beta = sigmoid(small)
    tri = (row_ids >= col_ids).astype(F32)
    decay_sum = mm_exact(tri, log_alpha)
    last = decay_sum[rows - 1 : rows, :]
    carried = aux[:, 4:5]
    growth = jnp.exp(decay_sum) * carried
    tail = jnp.exp(last - decay_sum) * aux[:, 5:6]
    keep = jnp.exp(last) * carried[rows - 1 : rows, :]
    return log_alpha, beta, decay_sum, growth, tail, keep, row_ids, col_ids


def transpose_lanes(values):
    return values.T


def conv_silu(ext, weights, aux, rows):
    total = ext(0) * weights[0]
    for offset in range(1, 4):
        total = total + ext(offset) * weights[offset] * aux[:, offset : offset + 1]
    return total


def forward_kernel(
    heads, place_ref, raw_ref, aux_ref, segrow_ref, conv_ref, scal_ref, gain_ref,
    mixed_ref, core_ref, inv_ref, upd_ref, st_ref, ext_ref, state_ref,
):
    step = pl.program_id(0)
    rows = raw_ref.shape[1]
    width = heads * HD

    @pl.when(step == 0)
    def _():
        ext_ref[0:8, :] = jnp.zeros_like(ext_ref[0:8, :])
        state_ref[...] = jnp.zeros_like(state_ref)

    aux = aux_ref[0]
    ext_ref[8 : 8 + rows, :] = raw_ref[0, :, 0 : 3 * width]
    small = raw_ref[0, :, 4 * width : 4 * width + LANES]
    _, beta, decay_sum, growth, tail, keep, row_ids, col_ids = chunk_gates(
        small, scal_ref, aux, heads
    )
    decay_rows = transpose_lanes(decay_sum)
    below = (row_ids >= col_ids) & (aux[:, 0:1] == segrow_ref[0, 0:1, :])
    strict = row_ids > col_ids
    eye = (row_ids == col_ids).astype(F32)

    def branch(index, head):
        lanes = slice(index * width + head * HD, index * width + (head + 1) * HD)
        weights = [conv_ref[4 * index + j : 4 * index + j + 1, head * HD : (head + 1) * HD] for j in range(4)]
        conv = conv_silu(lambda j: ext_ref[8 - j : 8 - j + rows, lanes], weights, aux, rows)
        return conv * sigmoid(conv)

    for head in range(heads):
        lanes = slice(head * HD, (head + 1) * HD)
        query = branch(0, head)
        query = query * (lax.rsqrt(jnp.sum(query * query, axis=-1, keepdims=True) + 1e-06) * SCALE)
        key = branch(1, head)
        key = key * lax.rsqrt(jnp.sum(key * key, axis=-1, keepdims=True) + 1e-06)
        value = branch(2, head)
        b_col = beta[:, heads + head : heads + head + 1]
        g_col = growth[:, head : head + 1]
        spread = decay_sum[:, head : head + 1] - decay_rows[head : head + 1, :]
        inside = jnp.exp(jnp.where(below, spread, -1e30))
        stacked = jnp.concatenate([key, query], axis=0).astype(BF)
        dots = mm_nt(stacked, key)
        power = jnp.where(strict, b_col * dots[:rows] * inside, 0.0)
        inverse = eye - jnp.where((row_ids // 2) == (col_ids // 2), power, 0.0)
        half = 2
        while half < rows:
            joint = ((row_ids // (2 * half)) == (col_ids // (2 * half))) & ((row_ids // half) != (col_ids // half))
            inv_low = inverse.astype(BF)
            inverse = inverse - mm(mm(inv_low, jnp.where(joint, power, 0.0)), inv_low)
            half *= 2
        state = state_ref[head]
        state_low = state.astype(BF)
        st_ref[0, head] = state_low
        applied = mm(stacked, state_low)
        rest = b_col * (value - g_col * applied[:rows])
        inv_low = inverse.astype(BF)
        inv_ref[0, head] = inv_low
        update = mm(inv_low, rest).astype(BF)
        upd_ref[0, :, lanes] = update
        core = g_col * applied[rows:] + mm(dots[rows:] * inside, update)
        state_ref[head] = keep[:, head : head + 1] * state + mm_tn(
            key * tail[:, head : head + 1], update
        )
        core_ref[0, :, lanes] = core
        outgate = raw_ref[0, :, 3 * width + head * HD : 3 * width + (head + 1) * HD]
        normed = core * lax.rsqrt(jnp.mean(core * core, axis=-1, keepdims=True) + 1e-05)
        mixed_ref[0, :, lanes] = (
            normed * gain_ref[0:1, lanes] * (outgate * sigmoid(outgate))
        ).astype(BF)
    ext_ref[0:8, :] = ext_ref[rows : rows + 8, :]


def backward_kernel(
    heads, place_ref, raw_ref, prev_ref, aux_ref, segrow_ref, conv_ref, scal_ref, gain_ref,
    dmix_ref, core_ref, inv_ref, upd_ref, st_ref,
    draw_ref, dconv_ref, dscal_ref, dgain_ref, ext_ref, dext_ref, dstate_ref,
):
    step = pl.program_id(0)
    rows = raw_ref.shape[1]
    width = heads * HD

    @pl.when(step == 0)
    def _():
        dext_ref[rows : rows + 8, :] = jnp.zeros_like(dext_ref[rows : rows + 8, :])
        dstate_ref[...] = jnp.zeros_like(dstate_ref)
        dconv_ref[...] = jnp.zeros_like(dconv_ref)
        dscal_ref[...] = jnp.zeros_like(dscal_ref)
        dgain_ref[...] = jnp.zeros_like(dgain_ref)

    @pl.when(step > 0)
    def _():
        dext_ref[rows : rows + 8, :] = dext_ref[0:8, :]

    aux = aux_ref[0]
    ext_ref[0:8, :] = prev_ref[0, :, 0 : 3 * width]
    ext_ref[8 : 8 + rows, :] = raw_ref[0, :, 0 : 3 * width]
    small = raw_ref[0, :, 4 * width : 4 * width + LANES]
    log_alpha, beta, decay_sum, growth, tail, keep, row_ids, col_ids = chunk_gates(
        small, scal_ref, aux, heads
    )
    decay_rows = transpose_lanes(decay_sum)
    below = (row_ids >= col_ids) & (aux[:, 0:1] == segrow_ref[0, 0:1, :])
    strict = row_ids > col_ids
    lane_ids = lax.broadcasted_iota(jnp.int32, (rows, LANES), 1)
    line_ids = lax.broadcasted_iota(jnp.int32, (LANES, rows), 0)
    last_row = lax.broadcasted_iota(jnp.int32, (rows, 1), 0) == rows - 1
    d_decay = jnp.zeros((rows, LANES), F32)
    d_beta = jnp.zeros((rows, LANES), F32)
    d_decay_lines = jnp.zeros((LANES, rows), F32)

    def branch(index, head):
        lanes = slice(index * width + head * HD, index * width + (head + 1) * HD)
        weights = [conv_ref[4 * index + j : 4 * index + j + 1, head * HD : (head + 1) * HD] for j in range(4)]
        conv = conv_silu(lambda j: ext_ref[8 - j : 8 - j + rows, lanes], weights, aux, rows)
        gate = sigmoid(conv)
        return conv * gate, gate * (1.0 + conv * (1.0 - gate))

    def conv_back(index, head, d_conv):
        lanes = slice(index * width + head * HD, index * width + (head + 1) * HD)
        own = slice(head * HD, (head + 1) * HD)
        dext_ref[0:rows, lanes] = d_conv
        total = d_conv * conv_ref[4 * index : 4 * index + 1, own]
        dconv_ref[4 * index : 4 * index + 1, own] += jnp.sum(
            d_conv * ext_ref[8 : 8 + rows, lanes], axis=0, keepdims=True
        )
        for j in range(1, 4):
            line = slice(4 * index + j, 4 * index + j + 1)
            total = total + dext_ref[j : j + rows, lanes] * conv_ref[line, own] * aux[:, 7 + j : 8 + j]
            dconv_ref[line, own] += jnp.sum(
                d_conv * ext_ref[8 - j : 8 - j + rows, lanes] * aux[:, j : j + 1],
                axis=0,
                keepdims=True,
            )
        draw_ref[0, :, lanes] = total.astype(BF)

    for head in range(heads):
        lanes = slice(head * HD, (head + 1) * HD)
        outgate = raw_ref[0, :, 3 * width + head * HD : 3 * width + (head + 1) * HD]
        gate = sigmoid(outgate)
        core = core_ref[0, :, lanes]
        inv_norm = lax.rsqrt(jnp.mean(core * core, axis=-1, keepdims=True) + 1e-05)
        normed = core * inv_norm
        d_mixed = dmix_ref[0, :, lanes].astype(F32)
        gain = gain_ref[0:1, lanes]
        d_silu = d_mixed * (outgate * gate)
        dgain_ref[0:1, lanes] += jnp.sum(d_silu * normed, axis=0, keepdims=True)
        draw_ref[0, :, 3 * width + head * HD : 3 * width + (head + 1) * HD] = (
            d_mixed * normed * gain * (gate * (1.0 + outgate * (1.0 - gate)))
        ).astype(BF)
        d_normed = d_silu * gain
        d_core = inv_norm * (
            d_normed - normed * jnp.mean(d_normed * normed, axis=-1, keepdims=True)
        )
        query_s, query_slope = branch(0, head)
        query_r = lax.rsqrt(jnp.sum(query_s * query_s, axis=-1, keepdims=True) + 1e-06)
        query_n = query_s * query_r
        query = query_n * SCALE
        key_s, key_slope = branch(1, head)
        key_r = lax.rsqrt(jnp.sum(key_s * key_s, axis=-1, keepdims=True) + 1e-06)
        key = key_s * key_r
        value, value_slope = branch(2, head)
        b_col = beta[:, heads + head : heads + head + 1]
        g_col = growth[:, head : head + 1]
        t_col = tail[:, head : head + 1]
        keep_one = keep[:, head : head + 1]
        spread = decay_sum[:, head : head + 1] - decay_rows[head : head + 1, :]
        inside = jnp.exp(jnp.where(below, spread, -1e30))
        inside_strict = jnp.where(strict, inside, 0.0)
        key_low = key.astype(BF)
        query_low = query.astype(BF)
        dots = mm_nt(jnp.concatenate([key_low, query_low], axis=0), key_low)
        inverse = inv_ref[0, head]
        update = upd_ref[0, :, lanes]
        state = st_ref[0, head]
        d_state = dstate_ref[head]
        d_state_low = d_state.astype(BF)
        d_core_low = d_core.astype(BF)
        weights_out = dots[rows:] * inside
        key_tail = key * t_col
        d_update = mm_tn(weights_out, d_core_low) + mm(key_tail, d_state_low)
        d_rest = mm_tn(inverse, d_update)
        d_rest_low = d_rest.astype(BF)
        both = mm_nt(jnp.concatenate([d_core_low, d_rest_low], axis=0), update)
        d_weights = both[:rows]
        d_power = -both[rows:]
        sides = mm_nt(jnp.concatenate([d_core_low, d_rest_low], axis=0), state)
        core_state = sides[:rows]
        rest_state = sides[rows:]
        d_tail_key = mm_nt(update, d_state_low)
        d_query_dots = d_weights * inside
        power_in = d_power * inside_strict
        d_key_dots = power_in * b_col
        key_dots = dots[:rows]
        reach = d_weights * weights_out + d_key_dots * key_dots
        d_beta_col = (
            jnp.sum(power_in * key_dots, axis=-1, keepdims=True)
            + jnp.sum(d_rest * value, axis=-1, keepdims=True)
            - g_col * jnp.sum(key * rest_state, axis=-1, keepdims=True)
        )
        d_growth = jnp.sum(query * core_state, axis=-1, keepdims=True) - b_col * jnp.sum(
            key * rest_state, axis=-1, keepdims=True
        )
        tail_part = t_col * jnp.sum(d_tail_key * key, axis=-1, keepdims=True)
        last_part = jnp.sum(tail_part, axis=0, keepdims=True) + keep_one * jnp.sum(
            jnp.sum(d_state * state.astype(F32), axis=-1, keepdims=True), axis=0, keepdims=True
        )
        d_sum_col = (
            jnp.sum(reach, axis=-1, keepdims=True)
            + g_col * d_growth
            - tail_part
            + jnp.where(last_row, last_part, 0.0)
        )
        d_decay = jnp.where(lane_ids == head, d_sum_col, d_decay)
        d_beta = jnp.where(lane_ids == heads + head, d_beta_col, d_beta)
        d_decay_lines = jnp.where(
            line_ids == head, jnp.sum(reach, axis=0, keepdims=True), d_decay_lines
        )
        scale_rest = -(b_col * g_col)
        d_value = b_col * d_rest
        d_query = g_col * core_state + mm(d_query_dots, key_low)
        d_key = (
            scale_rest * rest_state
            + t_col * d_tail_key
            + mm(d_key_dots, key_low)
            + mm_tn(jnp.concatenate([d_key_dots, d_query_dots], axis=0),
                    jnp.concatenate([key_low, query_low], axis=0))
        )
        dstate_ref[head] = keep_one * d_state + mm_tn(
            jnp.concatenate([query * g_col, key], axis=0),
            jnp.concatenate([d_core, scale_rest * d_rest], axis=0),
        )
        d_query_n = d_query * SCALE
        d_query_s = query_r * (
            d_query_n - query_n * jnp.sum(query_n * d_query_n, axis=-1, keepdims=True)
        )
        d_key_s = key_r * (d_key - key * jnp.sum(key * d_key, axis=-1, keepdims=True))
        conv_back(0, head, d_query_s * query_slope)
        conv_back(1, head, d_key_s * key_slope)
        conv_back(2, head, d_value * value_slope)

    d_decay = d_decay - transpose_lanes(d_decay_lines)
    upper = (row_ids <= col_ids).astype(F32)
    d_log = mm_exact(upper, d_decay)
    d_arg = d_log * scal_ref[0:1, :] * sigmoid(small + scal_ref[1:2, :])
    dscal_ref[0:1, :] += jnp.sum(d_log * log_alpha, axis=0, keepdims=True)
    dscal_ref[1:2, :] += jnp.sum(d_arg, axis=0, keepdims=True)
    draw_ref[0, :, 4 * width : 4 * width + LANES] = (
        d_arg + d_beta * beta * (1.0 - beta)
    ).astype(BF)


def mixer_shapes(raw):
    blocks, rows, total = raw.shape
    heads = (total - LANES) // (4 * HD)
    return blocks, rows, heads, heads * HD, total


def whole(shape):
    return pl.BlockSpec(shape, lambda c, place: (0,) * len(shape))


def mixer_forward(place, raw, aux, segrow, conv_rows, scal, gain):
    blocks, rows, heads, width, total = mixer_shapes(raw)
    at = lambda c, place: (place[c], 0, 0)
    seq = lambda c, place: (c, 0, 0)
    seq4 = lambda c, place: (c, 0, 0, 0)

    def body(*refs):
        forward_kernel(heads, *refs)

    return pl.pallas_call(
        body,
        grid_spec=pltpu.PrefetchScalarGridSpec(
            num_scalar_prefetch=1,
            grid=(blocks,),
            in_specs=[
                pl.BlockSpec((1, rows, total), at),
                pl.BlockSpec((1, rows, 16), seq),
                pl.BlockSpec((1, 8, rows), seq),
                whole(conv_rows.shape),
                whole(scal.shape),
                whole(gain.shape),
            ],
            out_specs=[
                pl.BlockSpec((1, rows, width), at),
                pl.BlockSpec((1, rows, width), seq),
                pl.BlockSpec((1, heads, rows, rows), seq4),
                pl.BlockSpec((1, rows, width), seq),
                pl.BlockSpec((1, heads, HD, HD), seq4),
            ],
            scratch_shapes=[
                pltpu.VMEM((rows + 8, 3 * width), F32),
                pltpu.VMEM((heads, HD, HD), F32),
            ],
        ),
        out_shape=[
            jax.ShapeDtypeStruct((blocks, rows, width), BF),
            jax.ShapeDtypeStruct((blocks, rows, width), F32),
            jax.ShapeDtypeStruct((blocks, heads, rows, rows), BF),
            jax.ShapeDtypeStruct((blocks, rows, width), BF),
            jax.ShapeDtypeStruct((blocks, heads, HD, HD), BF),
        ],
        compiler_params=pltpu.CompilerParams(
            dimension_semantics=("arbitrary",), vmem_limit_bytes=48 * 1024 * 1024
        ),
        cost_estimate=pl.CostEstimate(
            flops=blocks * heads * 2 * HD * HD * HD * 80, bytes_accessed=8_000_000, transcendentals=0
        ),
        name="mixer_forward",
    )(place, raw, aux, segrow, conv_rows, scal, gain)


def mixer_backward(place, raw, aux, segrow, conv_rows, scal, gain, d_mixed, saved):
    blocks, rows, heads, width, total = mixer_shapes(raw)
    core, inverse, update, states = saved
    back = lambda c: blocks - 1 - c
    at = lambda c, place: (place[back(c)], 0, 0)
    before = lambda c, place: (place[jnp.maximum(back(c) - 1, 0)], rows // 8 - 1, 0)
    seq = lambda c, place: (back(c), 0, 0)
    seq4 = lambda c, place: (back(c), 0, 0, 0)

    def body(*refs):
        backward_kernel(heads, *refs)

    return pl.pallas_call(
        body,
        grid_spec=pltpu.PrefetchScalarGridSpec(
            num_scalar_prefetch=1,
            grid=(blocks,),
            in_specs=[
                pl.BlockSpec((1, rows, total), at),
                pl.BlockSpec((1, 8, total), before),
                pl.BlockSpec((1, rows, 16), seq),
                pl.BlockSpec((1, 8, rows), seq),
                whole(conv_rows.shape),
                whole(scal.shape),
                whole(gain.shape),
                pl.BlockSpec((1, rows, width), at),
                pl.BlockSpec((1, rows, width), seq),
                pl.BlockSpec((1, heads, rows, rows), seq4),
                pl.BlockSpec((1, rows, width), seq),
                pl.BlockSpec((1, heads, HD, HD), seq4),
            ],
            out_specs=[
                pl.BlockSpec((1, rows, total), at),
                whole((16, width)),
                whole((8, LANES)),
                whole((8, width)),
            ],
            scratch_shapes=[
                pltpu.VMEM((rows + 8, 3 * width), F32),
                pltpu.VMEM((rows + 8, 3 * width), F32),
                pltpu.VMEM((heads, HD, HD), F32),
            ],
        ),
        out_shape=[
            jax.ShapeDtypeStruct((blocks, rows, total), BF),
            jax.ShapeDtypeStruct((16, width), F32),
            jax.ShapeDtypeStruct((8, LANES), F32),
            jax.ShapeDtypeStruct((8, width), F32),
        ],
        compiler_params=pltpu.CompilerParams(
            dimension_semantics=("arbitrary",), vmem_limit_bytes=48 * 1024 * 1024
        ),
        cost_estimate=pl.CostEstimate(
            flops=blocks * heads * 2 * HD * HD * HD * 160, bytes_accessed=12_000_000, transcendentals=0
        ),
        name="mixer_backward",
    )(place, raw, raw, aux, segrow, conv_rows, scal, gain, d_mixed, core, inverse, update, states)


def hop(values, bit):
    size = lax.axis_size("head")
    return lax.ppermute(values, "head", [(i, i ^ bit) for i in range(size)])


def gather(values):
    if lax.axis_size("head") != 4:
        return lax.all_gather(values, "head", axis=0, tiled=False)
    half = values.shape[0] // 2
    from_x = hop(values, 1)
    from_y = hop(values, 2)
    far_a = hop(from_y[:half], 1)
    far_b = hop(from_x[half:], 2)
    full = jnp.concatenate([values, from_x, from_y, far_a, far_b], axis=0)
    return full.reshape((4,) + values.shape)


def scatter(parts):
    if lax.axis_size("head") != 4:
        return lax.psum_scatter(
            parts.astype(BF), "head", scatter_dimension=0, tiled=False
        ).astype(F32)
    half = parts.shape[1] // 2
    low = parts.astype(BF)
    top, end = low[:, :half], low[:, half:]
    in_x = hop(jnp.stack([top[1], top[3]]), 1).astype(F32)
    in_y = hop(jnp.stack([end[2], end[3]]), 2).astype(F32)
    pass_y = (parts[2, :half] + in_x[1]).astype(BF)
    pass_x = (parts[1, half:] + in_y[1]).astype(BF)
    last_y = hop(pass_y, 2).astype(F32)
    last_x = hop(pass_x, 1).astype(F32)
    return jnp.concatenate(
        [parts[0, :half] + in_x[0] + last_y, parts[0, half:] + in_y[0] + last_x], axis=0
    )


def block_places(size):
    base = lax.iota(jnp.int32, size)
    if size != 4:
        return base
    return base ^ lax.axis_index("head").astype(jnp.int32)


def contract_rows(left, right):
    return lax.dot_general(left, right, (((0,), (0,)), ((), ())), preferred_element_type=F32)


def contract_cols(left, right):
    return lax.dot_general(left, right, (((1,), (1,)), ((), ())), preferred_element_type=F32)


def times(left, right):
    return jnp.dot(left, right, preferred_element_type=F32)


def sequence_facts(doc_lengths, blocks, rows):
    span = blocks * rows
    ends = jnp.cumsum(doc_lengths, axis=-1)
    places = lax.iota(jnp.int32, span)
    segment = jnp.sum((places[None, :, None] >= ends[:, None, :]).astype(jnp.int32), axis=-1)
    columns = [segment]
    for j in range(1, 4):
        columns.append(
            (jnp.pad(segment, ((0, 0), (j, 0)), constant_values=-1)[:, :-j] == segment)
        )
    by_chunk = segment.reshape(-1, blocks, rows)
    prior = jnp.pad(by_chunk[:, :-1, -1], ((0, 0), (1, 0)), constant_values=-1)
    columns.append((by_chunk == prior[:, :, None]).reshape(segment.shape))
    columns.append((by_chunk == by_chunk[:, :, -1:]).reshape(segment.shape))
    columns += [jnp.zeros_like(segment)] * 2
    for j in range(1, 4):
        columns.append(
            (jnp.pad(segment, ((0, 0), (0, j)), constant_values=-1)[:, j:] == segment)
        )
    columns += [jnp.zeros_like(segment)] * (16 - len(columns))
    aux = jnp.stack([item.astype(F32) for item in columns], axis=-1)
    aux = aux.reshape(-1, blocks, rows, 16)
    lines = jnp.broadcast_to(by_chunk.astype(F32)[:, :, None, :], by_chunk.shape[:2] + (8, rows))
    return aux, lines


def on_device(
    tokens, cotangent, token_counts, doc_lengths, norm_in, w_query, w_key, w_value, w_outgate,
    w_decay, w_beta, conv_weight, decay_log, dt_bias, gain_out, w_out, norm_mid, w_gate, w_up,
    w_down,
):
    micro_count, rows, width = tokens.shape
    blocks = lax.axis_size("head")
    span = rows * blocks
    heads = decay_log.shape[0]
    own = heads * HD
    micros = range(micro_count)
    my_places = lax.axis_index("head") * rows + lax.iota(jnp.int32, rows)
    place = block_places(blocks)
    aux, lines = sequence_facts(doc_lengths[:, 0], blocks, rows)
    conv_rows = jnp.pad(conv_weight.reshape(12, own), ((0, 4), (0, 0)))
    scal = jnp.zeros((8, LANES), F32)
    scal = scal.at[0, :heads].set(-jnp.exp(decay_log)).at[1, :heads].set(dt_bias)
    gain_row = jnp.broadcast_to(gain_out[None], (8, own))
    w_in = jnp.concatenate(
        [w_query, w_key, w_value, w_outgate, w_decay, w_beta,
         jnp.zeros((width, LANES - 2 * heads), BF)], axis=1
    )
    ffn_gate = lax.all_gather(w_gate, "dp", axis=0, tiled=True)
    ffn_up = lax.all_gather(w_up, "dp", axis=0, tiled=True)
    ffn_down = lax.all_gather(w_down, "dp", axis=0, tiled=True)

    inputs, grads, pulls_in, full_in, full_grad = [], [], [], [], []
    for m in micros:
        x = tokens[m].astype(F32)
        normed, pull = jax.vjp(norm_rows, x, norm_in)
        live = (my_places < token_counts[m, 0]).astype(F32)
        inputs.append(x)
        pulls_in.append(pull)
        full_in.append(gather(normed.astype(BF)))
        grads.append(cotangent[m].astype(F32) * live[:, None])
    raws, saved, mixed, resids, pulls_mid, full_mid = [], [], [], [], [], []
    for m in micros:
        raw = times(full_in[m].reshape(span, width), w_in).reshape(blocks, rows, 4 * own + LANES)
        mixed_m, *saved_m = mixer_forward(place, raw, aux[m], lines[m], conv_rows, scal, gain_row)
        raws.append(raw)
        saved.append(saved_m)
        mixed.append(mixed_m.reshape(span, own))
        attn = scatter(times(mixed[m], w_out).reshape(blocks, rows, width))
        full_grad.append(gather(grads[m].astype(BF)).reshape(span, width))
        resid = inputs[m] + attn
        normed, pull = jax.vjp(norm_rows, resid, norm_mid)
        resids.append(resid)
        pulls_mid.append(pull)
        full_mid.append(gather(normed.astype(BF)).reshape(span, width))
    results, acts, gates, ups, resid_grads, full_resid = [], [], [], [], [], []
    gain_mid = jnp.zeros_like(norm_mid)
    for m in micros:
        gate = times(full_mid[m], ffn_gate)
        upward = times(full_mid[m], ffn_up)
        act_full, act_pull = jax.vjp(swiglu, gate, upward)
        act = act_full.astype(BF)
        d_gate, d_up = act_pull(times(full_grad[m], ffn_down))
        d_gate, d_up = d_gate.astype(BF), d_up.astype(BF)
        d_mid = scatter(
            (contract_cols(d_gate, ffn_gate) + contract_cols(d_up, ffn_up)).reshape(
                blocks, rows, width
            )
        )
        ffn = scatter(contract_cols(act, ffn_down).reshape(blocks, rows, width))
        results.append((resids[m] + ffn).astype(BF))
        d_resid, d_norm = pulls_mid[m](d_mid)
        d_resid = grads[m] + d_resid
        gain_mid = gain_mid + d_norm
        resid_grads.append(d_resid)
        full_resid.append(gather(d_resid.astype(BF)).reshape(span, width))
        acts.append(act)
        gates.append(d_gate)
        ups.append(d_up)

    def over_micros(left, right):
        return contract_rows(
            jnp.concatenate(left, axis=0), jnp.concatenate(right, axis=0)
        ).astype(BF)

    def share(term):
        return lax.psum_scatter(term, "dp", scatter_dimension=0, tiled=True).astype(F32)

    grad_gate = share(over_micros(full_mid, gates))
    grad_up = share(over_micros(full_mid, ups))
    grad_down = share(over_micros(full_grad, acts))
    grad_out = share(over_micros(full_resid, mixed)).T

    d_raws, input_grads = [], []
    gain_in = jnp.zeros_like(norm_in)
    small_sums = None
    for m in micros:
        d_mixed = contract_cols(full_resid[m], w_out).reshape(blocks, rows, own)
        d_raw, *d_params = mixer_backward(
            place, raws[m], aux[m], lines[m], conv_rows, scal, gain_row, d_mixed, saved[m]
        )
        small_sums = d_params if small_sums is None else [
            total + item for total, item in zip(small_sums, d_params)
        ]
        d_raws.append(d_raw.reshape(span, 4 * own + LANES))
        d_normed = scatter(contract_cols(d_raws[m], w_in).reshape(blocks, rows, width))
        d_inputs, d_norm = pulls_in[m](d_normed)
        input_grads.append((d_inputs + resid_grads[m]).astype(BF))
        gain_in = gain_in + d_norm
    flat_in = [item.reshape(span, width) for item in full_in]
    grad_in = share(over_micros(flat_in, d_raws))
    gain_sums = lax.psum((gain_in, gain_mid), ("dp", "head"))
    param_sums = lax.psum(
        (small_sums[0][:12], small_sums[1][:2, :heads], small_sums[2][0]), "dp"
    )
    return (
        jnp.stack(results),
        jnp.stack(input_grads),
        gain_sums[0],
        grad_in[:, :own],
        grad_in[:, own : 2 * own],
        grad_in[:, 2 * own : 3 * own],
        grad_in[:, 3 * own : 4 * own],
        grad_in[:, 4 * own : 4 * own + heads],
        grad_in[:, 4 * own + heads : 4 * own + 2 * heads],
        param_sums[0].reshape(conv_weight.shape),
        param_sums[1][0],
        param_sums[1][1],
        param_sums[2],
        grad_out,
        gain_sums[1],
        grad_gate,
        grad_up,
        grad_down,
    )


def solution(mesh):
    return jax.shard_map(
        on_device,
        mesh=mesh,
        in_specs=(
            P(None, ("dp", "head"), None),
            P(None, ("dp", "head"), None),
            P(None, "dp"),
            P(None, "dp", None),
            P(),
            P(None, "head"),
            P(None, "head"),
            P(None, "head"),
            P(None, "head"),
            P(None, "head"),
            P(None, "head"),
            P(None, None, "head"),
            P("head"),
            P("head"),
            P("head"),
            P("head", None),
            P(),
            P("dp", "head"),
            P("dp", "head"),
            P("dp", "head"),
        ),
        out_specs=(
            P(None, ("dp", "head"), None),
            P(None, ("dp", "head"), None),
            P(),
            P("dp", "head"),
            P("dp", "head"),
            P("dp", "head"),
            P("dp", "head"),
            P("dp", "head"),
            P("dp", "head"),
            P(None, None, "head"),
            P("head"),
            P("head"),
            P("head"),
            P("head", "dp"),
            P(),
            P("dp", "head"),
            P("dp", "head"),
            P("dp", "head"),
        ),
        check_vma=False,
    )
```

```python
import jax
import jax.numpy as jnp
from jax import lax
from jax.experimental import pallas as pl
from jax.experimental.pallas import tpu as pltpu
from jax.sharding import PartitionSpec as P

HD = 128
LANES = 128
SCALE = HD ** (-0.5)
BF = jnp.bfloat16
F32 = jnp.float32
FORWARD_COST = 735_000_000
BACKWARD_COST = 1_650_000_000


def norm_rows(values, gain):
    return values * lax.rsqrt(jnp.mean(values * values, axis=-1, keepdims=True) + 1e-05) * gain


def swiglu(gate, upward):
    return jax.nn.silu(gate) * upward


def mm(left, right):
    return jnp.dot(left.astype(BF), right.astype(BF), preferred_element_type=F32)


def mm_nt(left, right):
    return lax.dot_general(
        left.astype(BF), right.astype(BF), (((1,), (1,)), ((), ())), preferred_element_type=F32
    )


def mm_tn(left, right):
    return lax.dot_general(
        left.astype(BF), right.astype(BF), (((0,), (0,)), ((), ())), preferred_element_type=F32
    )


def mm_exact(left, right):
    return jnp.dot(left, right, preferred_element_type=F32, precision=lax.Precision.HIGHEST)


def sigmoid(values):
    return 1.0 / (1.0 + jnp.exp(-values))


def softplus(values):
    return jnp.maximum(values, 0.0) + jnp.log1p(jnp.exp(-jnp.abs(values)))


def chunk_masks(rows):
    row_ids = lax.broadcasted_iota(jnp.int32, (rows, rows), 0)
    col_ids = lax.broadcasted_iota(jnp.int32, (rows, rows), 1)
    return row_ids, col_ids


def chunk_gates(small, scal_ref, aux, tri):
    rows = small.shape[0]
    log_alpha = scal_ref[0:1, :] * softplus(small + scal_ref[1:2, :])
    beta = sigmoid(small)
    decay_sum = mm_exact(tri, log_alpha)
    last = decay_sum[rows - 1 : rows, :]
    carried = aux[:, 4:5]
    growth = jnp.exp(decay_sum) * carried
    tail = jnp.exp(last - decay_sum) * aux[:, 5:6]
    keep = jnp.exp(last) * carried[rows - 1 : rows, :]
    return log_alpha, beta, decay_sum, growth, tail, keep


def conv_of(ext_ref, conv_ref, aux, m, index, head, rows, width):
    lanes = slice(index * width + head * HD, index * width + (head + 1) * HD)
    own = slice(head * HD, (head + 1) * HD)
    total = ext_ref[m, 8 : 8 + rows, lanes] * conv_ref[4 * index : 4 * index + 1, own]
    for j in range(1, 4):
        line = slice(4 * index + j, 4 * index + j + 1)
        total = total + ext_ref[m, 8 - j : 8 - j + rows, lanes] * conv_ref[line, own] * aux[:, j : j + 1]
    return total


def invert_unit_lower(powers, row_ids, col_ids):
    rows = row_ids.shape[0]
    eye = (row_ids == col_ids).astype(F32)
    pair = (row_ids // 2) == (col_ids // 2)
    inverses = [eye - jnp.where(pair, power, 0.0) for power in powers]
    half = 2
    while half < rows:
        joint = ((row_ids // (2 * half)) == (col_ids // (2 * half))) & (
            (row_ids // half) != (col_ids // half)
        )
        lows = [inverse.astype(BF) for inverse in inverses]
        firsts = [mm(low, jnp.where(joint, power, 0.0)) for low, power in zip(lows, powers)]
        inverses = [
            inverse - mm(first, low) for inverse, first, low in zip(inverses, firsts, lows)
        ]
        half *= 2
    return [inverse.astype(BF) for inverse in inverses]


def forward_kernel(
    heads, place_ref, raw_ref, aux_ref, segrow_ref, conv_ref, scal_ref, gain_ref,
    mixed_ref, core_ref, inv_ref, upd_ref, st_ref, ext_ref, state_ref,
):
    step = pl.program_id(0)
    group, rows = raw_ref.shape[1:3]
    width = heads * HD
    row_ids, col_ids = chunk_masks(rows)
    tri = (row_ids >= col_ids).astype(F32)
    strict = row_ids > col_ids

    @pl.when(step == 0)
    def _():
        ext_ref[:, 0:8, :] = jnp.zeros((group, 8, 3 * width), F32)
        state_ref[...] = jnp.zeros_like(state_ref)

    ext_ref[:, 8 : 8 + rows, :] = raw_ref[0, :, :, 0 : 3 * width]
    chains = [(m, h) for m in range(group) for h in range(heads)]
    stacked, values, powers, outs, betas, growths, tails, keeps = [], [], [], [], [], [], [], []
    for m in range(group):
        aux = aux_ref[m, 0]
        small = raw_ref[0, m, :, 4 * width : 4 * width + LANES]
        _, beta, decay_sum, growth, tail, keep = chunk_gates(small, scal_ref, aux, tri)
        decay_rows = decay_sum.T
        below = (row_ids >= col_ids) & (aux[:, 0:1] == segrow_ref[m, 0, 0:1, :])
        for head in range(heads):
            query = conv_of(ext_ref, conv_ref, aux, m, 0, head, rows, width)
            query = query * sigmoid(query)
            query = query * (
                lax.rsqrt(jnp.sum(query * query, axis=-1, keepdims=True) + 1e-06) * SCALE
            )
            key = conv_of(ext_ref, conv_ref, aux, m, 1, head, rows, width)
            key = key * sigmoid(key)
            key = key * lax.rsqrt(jnp.sum(key * key, axis=-1, keepdims=True) + 1e-06)
            value = conv_of(ext_ref, conv_ref, aux, m, 2, head, rows, width)
            value = value * sigmoid(value)
            b_col = beta[:, heads + head : heads + head + 1]
            spread = decay_sum[:, head : head + 1] - decay_rows[head : head + 1, :]
            inside = jnp.exp(jnp.where(below, spread, -1e30))
            both = jnp.concatenate([key, query], axis=0).astype(BF)
            dots = mm_nt(both, both[:rows])
            stacked.append(both)
            values.append(value)
            powers.append(jnp.where(strict, b_col * dots[:rows] * inside, 0.0))
            outs.append((dots[rows:] * inside).astype(BF))
            betas.append(b_col)
            growths.append(growth[:, head : head + 1])
            tails.append(tail[:, head : head + 1])
            keeps.append(keep[:, head : head + 1])
    inverses = invert_unit_lower(powers, row_ids, col_ids)
    states = [state_ref[m, h] for m, h in chains]
    lows = [state.astype(BF) for state in states]
    applied = [mm(both, low) for both, low in zip(stacked, lows)]
    updates = []
    for i, (m, h) in enumerate(chains):
        st_ref[0, m, h] = lows[i]
        inv_ref[0, m, h] = inverses[i]
        rest = betas[i] * (values[i] - growths[i] * applied[i][:rows])
        updates.append(mm(inverses[i], rest).astype(BF))
    for i, (m, h) in enumerate(chains):
        lanes = slice(h * HD, (h + 1) * HD)
        upd_ref[0, m, :, lanes] = updates[i]
        state_ref[m, h] = keeps[i] * states[i] + mm_tn(
            stacked[i][:rows].astype(F32) * tails[i], updates[i]
        )
        core = growths[i] * applied[i][rows:] + mm(outs[i], updates[i])
        core_ref[0, m, :, lanes] = core
        outgate = raw_ref[0, m, :, 3 * width + h * HD : 3 * width + (h + 1) * HD]
        normed = core * lax.rsqrt(jnp.mean(core * core, axis=-1, keepdims=True) + 1e-05)
        mixed_ref[0, m, :, lanes] = (
            normed * gain_ref[0:1, lanes] * (outgate * sigmoid(outgate))
        ).astype(BF)
    ext_ref[:, 0:8, :] = ext_ref[:, rows : rows + 8, :]


def backward_kernel(
    heads, place_ref, raw_ref, prev_ref, aux_ref, segrow_ref, conv_ref, scal_ref, gain_ref,
    dmix_ref, core_ref, inv_ref, upd_ref, st_ref,
    draw_ref, dconv_ref, dscal_ref, dgain_ref, ext_ref, dext_ref, dstate_ref,
):
    step = pl.program_id(0)
    group, rows = raw_ref.shape[1:3]
    width = heads * HD

    @pl.when(step == 0)
    def _():
        dext_ref[:, rows : rows + 8, :] = jnp.zeros((group, 8, 3 * width), F32)
        dstate_ref[...] = jnp.zeros_like(dstate_ref)
        dconv_ref[...] = jnp.zeros_like(dconv_ref)
        dscal_ref[...] = jnp.zeros_like(dscal_ref)
        dgain_ref[...] = jnp.zeros_like(dgain_ref)

    @pl.when(step > 0)
    def _():
        dext_ref[:, rows : rows + 8, :] = dext_ref[:, 0:8, :]

    ext_ref[:, 0:8, :] = prev_ref[0, :, :, 0 : 3 * width]
    ext_ref[:, 8 : 8 + rows, :] = raw_ref[0, :, :, 0 : 3 * width]
    row_ids, col_ids = chunk_masks(rows)
    tri = (row_ids >= col_ids).astype(F32)
    upper = (row_ids <= col_ids).astype(F32)
    strict = row_ids > col_ids
    lane_ids = lax.broadcasted_iota(jnp.int32, (rows, LANES), 1)
    line_ids = lax.broadcasted_iota(jnp.int32, (LANES, rows), 0)
    last_row = lax.broadcasted_iota(jnp.int32, (rows, 1), 0) == rows - 1

    def conv_back(m, index, head, aux, d_conv):
        lanes = slice(index * width + head * HD, index * width + (head + 1) * HD)
        own = slice(head * HD, (head + 1) * HD)
        dext_ref[m, 0:rows, lanes] = d_conv
        total = d_conv * conv_ref[4 * index : 4 * index + 1, own]
        dconv_ref[4 * index : 4 * index + 1, own] += jnp.sum(
            d_conv * ext_ref[m, 8 : 8 + rows, lanes], axis=0, keepdims=True
        )
        for j in range(1, 4):
            line = slice(4 * index + j, 4 * index + j + 1)
            total = total + dext_ref[m, j : j + rows, lanes] * conv_ref[line, own] * aux[:, 7 + j : 8 + j]
            dconv_ref[line, own] += jnp.sum(
                d_conv * ext_ref[m, 8 - j : 8 - j + rows, lanes] * aux[:, j : j + 1],
                axis=0,
                keepdims=True,
            )
        draw_ref[0, m, :, lanes] = total.astype(BF)

    for m in range(group):
        aux = aux_ref[m, 0]
        small = raw_ref[0, m, :, 4 * width : 4 * width + LANES]
        log_alpha, beta, decay_sum, growth, tail, keep = chunk_gates(small, scal_ref, aux, tri)
        decay_rows = decay_sum.T
        below = (row_ids >= col_ids) & (aux[:, 0:1] == segrow_ref[m, 0, 0:1, :])
        d_decay = jnp.zeros((rows, LANES), F32)
        d_beta = jnp.zeros((rows, LANES), F32)
        d_decay_lines = jnp.zeros((LANES, rows), F32)
        everyone = range(heads)
        own_lanes = [slice(h * HD, (h + 1) * HD) for h in everyone]
        b_cols = [beta[:, heads + h : heads + h + 1] for h in everyone]
        g_cols = [growth[:, h : h + 1] for h in everyone]
        t_cols = [tail[:, h : h + 1] for h in everyone]
        keeps = [keep[:, h : h + 1] for h in everyone]
        d_cores, queries, keys, values = [], [], [], []
        for h in everyone:
            lanes = own_lanes[h]
            gate_lanes = slice(3 * width + h * HD, 3 * width + (h + 1) * HD)
            outgate = raw_ref[0, m, :, gate_lanes]
            gate = sigmoid(outgate)
            core = core_ref[0, m, :, lanes]
            inv_norm = lax.rsqrt(jnp.mean(core * core, axis=-1, keepdims=True) + 1e-05)
            normed = core * inv_norm
            d_mixed = dmix_ref[0, m, :, lanes].astype(F32)
            gain = gain_ref[0:1, lanes]
            d_silu = d_mixed * (outgate * gate)
            dgain_ref[0:1, lanes] += jnp.sum(d_silu * normed, axis=0, keepdims=True)
            draw_ref[0, m, :, gate_lanes] = (
                d_mixed * normed * gain * (gate * (1.0 + outgate * (1.0 - gate)))
            ).astype(BF)
            d_normed = d_silu * gain
            d_cores.append(
                (inv_norm * (d_normed - normed * jnp.mean(d_normed * normed, axis=-1, keepdims=True))).astype(BF)
            )
            parts = []
            for index in range(3):
                conv = conv_of(ext_ref, conv_ref, aux, m, index, h, rows, width)
                gate = sigmoid(conv)
                act = conv * gate
                slope = gate * (1.0 + conv * (1.0 - gate))
                if index == 2:
                    parts.append((act, slope))
                else:
                    root = lax.rsqrt(jnp.sum(act * act, axis=-1, keepdims=True) + 1e-06)
                    parts.append((act * root, slope * root))
            queries.append(parts[0])
            keys.append(parts[1])
            values.append(parts[2])
        insides = [
            jnp.exp(jnp.where(below, decay_sum[:, h : h + 1] - decay_rows[h : h + 1, :], -1e30))
            for h in everyone
        ]
        key_lows = [keys[h][0].astype(BF) for h in everyone]
        query_lows = [(queries[h][0] * SCALE).astype(BF) for h in everyone]
        dots = [
            mm_nt(jnp.concatenate([key_lows[h], query_lows[h]], axis=0), key_lows[h])
            for h in everyone
        ]
        updates = [upd_ref[0, m, :, own_lanes[h]] for h in everyone]
        states = [st_ref[0, m, h] for h in everyone]
        d_states = [dstate_ref[m, h] for h in everyone]
        d_state_lows = [item.astype(BF) for item in d_states]
        outs = [dots[h][rows:] * insides[h] for h in everyone]
        d_updates = [
            mm_tn(outs[h], d_cores[h]) + mm(keys[h][0] * t_cols[h], d_state_lows[h])
            for h in everyone
        ]
        d_rests = [mm_tn(inv_ref[0, m, h], d_updates[h]) for h in everyone]
        pairs = [
            jnp.concatenate([d_cores[h], d_rests[h].astype(BF)], axis=0) for h in everyone
        ]
        boths = [mm_nt(pairs[h], updates[h]) for h in everyone]
        sides = [mm_nt(pairs[h], states[h]) for h in everyone]
        d_tail_keys = [mm_nt(updates[h], d_state_lows[h]) for h in everyone]
        for h in everyone:
            key, query = keys[h][0], queries[h][0]
            d_weights, d_power = boths[h][:rows], -boths[h][rows:]
            core_state, rest_state = sides[h][:rows], sides[h][rows:]
            key_dots = dots[h][:rows]
            d_query_dots = d_weights * insides[h]
            power_in = jnp.where(strict, d_power * insides[h], 0.0)
            d_key_dots = power_in * b_cols[h]
            reach = d_weights * outs[h] + d_key_dots * key_dots
            key_rest = jnp.sum(key * rest_state, axis=-1, keepdims=True)
            d_beta_col = (
                jnp.sum(power_in * key_dots, axis=-1, keepdims=True)
                + jnp.sum(d_rests[h] * values[h][0], axis=-1, keepdims=True)
                - g_cols[h] * key_rest
            )
            d_growth = SCALE * jnp.sum(query * core_state, axis=-1, keepdims=True) - b_cols[h] * key_rest
            tail_part = t_cols[h] * jnp.sum(d_tail_keys[h] * key, axis=-1, keepdims=True)
            last_part = jnp.sum(tail_part, axis=0, keepdims=True) + keeps[h] * jnp.sum(
                jnp.sum(d_states[h] * states[h].astype(F32), axis=0, keepdims=True),
                axis=-1,
                keepdims=True,
            )
            d_sum_col = (
                jnp.sum(reach, axis=-1, keepdims=True)
                + g_cols[h] * d_growth
                - tail_part
                + jnp.where(last_row, last_part, 0.0)
            )
            d_decay = jnp.where(lane_ids == h, d_sum_col, d_decay)
            d_beta = jnp.where(lane_ids == heads + h, d_beta_col, d_beta)
            d_decay_lines = jnp.where(
                line_ids == h, jnp.sum(reach, axis=0, keepdims=True), d_decay_lines
            )
            scale_rest = -(b_cols[h] * g_cols[h])
            dot_grads = jnp.concatenate([d_key_dots, d_query_dots], axis=0).astype(BF)
            by_key = mm(dot_grads, key_lows[h])
            d_query = (g_cols[h] * core_state + by_key[rows:]) * SCALE
            d_key = (
                scale_rest * rest_state
                + t_cols[h] * d_tail_keys[h]
                + by_key[:rows]
                + mm_tn(dot_grads, jnp.concatenate([key_lows[h], query_lows[h]], axis=0))
            )
            dstate_ref[m, h] = keeps[h] * d_states[h] + mm_tn(
                jnp.concatenate([query * (SCALE * g_cols[h]), key * scale_rest], axis=0), pairs[h]
            )
            conv_back(
                m, 0, h, aux,
                queries[h][1] * (d_query - query * jnp.sum(query * d_query, axis=-1, keepdims=True)),
            )
            conv_back(
                m, 1, h, aux,
                keys[h][1] * (d_key - key * jnp.sum(key * d_key, axis=-1, keepdims=True)),
            )
            conv_back(m, 2, h, aux, b_cols[h] * d_rests[h] * values[h][1])
        d_log = mm_exact(upper, d_decay - d_decay_lines.T)
        d_arg = d_log * scal_ref[0:1, :] * sigmoid(small + scal_ref[1:2, :])
        dscal_ref[0:1, :] += jnp.sum(d_log * log_alpha, axis=0, keepdims=True)
        dscal_ref[1:2, :] += jnp.sum(d_arg, axis=0, keepdims=True)
        draw_ref[0, m, :, 4 * width : 4 * width + LANES] = (
            d_arg + d_beta * beta * (1.0 - beta)
        ).astype(BF)


def mixer_shapes(raw):
    blocks, group, rows, total = raw.shape
    heads = (total - LANES) // (4 * HD)
    return blocks, group, rows, heads, heads * HD, total


def whole(shape):
    return pl.BlockSpec(shape, lambda c, place: (0,) * len(shape))


PARAMS = dict(dimension_semantics=("arbitrary",), vmem_limit_bytes=56 * 1024 * 1024)


def mixer_forward(place, raw, aux, segrow, conv_rows, scal, gain):
    blocks, group, rows, heads, width, total = mixer_shapes(raw)
    at = lambda c, place: (place[c], 0, 0, 0)
    seq = lambda c, place: (c, 0, 0, 0)
    seq5 = lambda c, place: (c, 0, 0, 0, 0)
    fact = lambda c, place: (0, c, 0, 0)

    def body(*refs):
        forward_kernel(heads, *refs)

    return pl.pallas_call(
        body,
        grid_spec=pltpu.PrefetchScalarGridSpec(
            num_scalar_prefetch=1,
            grid=(blocks,),
            in_specs=[
                pl.BlockSpec((1, group, rows, total), at),
                pl.BlockSpec((group, 1, rows, 16), fact),
                pl.BlockSpec((group, 1, 8, rows), fact),
                whole(conv_rows.shape),
                whole(scal.shape),
                whole(gain.shape),
            ],
            out_specs=[
                pl.BlockSpec((1, group, rows, width), at),
                pl.BlockSpec((1, group, rows, width), seq),
                pl.BlockSpec((1, group, heads, rows, rows), seq5),
                pl.BlockSpec((1, group, rows, width), seq),
                pl.BlockSpec((1, group, heads, HD, HD), seq5),
            ],
            scratch_shapes=[
                pltpu.VMEM((group, rows + 8, 3 * width), F32),
                pltpu.VMEM((group, heads, HD, HD), F32),
            ],
        ),
        out_shape=[
            jax.ShapeDtypeStruct((blocks, group, rows, width), BF),
            jax.ShapeDtypeStruct((blocks, group, rows, width), F32),
            jax.ShapeDtypeStruct((blocks, group, heads, rows, rows), BF),
            jax.ShapeDtypeStruct((blocks, group, rows, width), BF),
            jax.ShapeDtypeStruct((blocks, group, heads, HD, HD), BF),
        ],
        compiler_params=pltpu.CompilerParams(**PARAMS),
        cost_estimate=pl.CostEstimate(
            flops=FORWARD_COST * blocks * group * heads, bytes_accessed=8_000_000, transcendentals=0
        ),
        name="mixer_forward",
    )(place, raw, aux, segrow, conv_rows, scal, gain)


def mixer_backward(place, raw, aux, segrow, conv_rows, scal, gain, d_mixed, saved):
    blocks, group, rows, heads, width, total = mixer_shapes(raw)
    core, inverse, update, states = saved
    back = lambda c: blocks - 1 - c
    at = lambda c, place: (place[back(c)], 0, 0, 0)
    before = lambda c, place: (place[jnp.maximum(back(c) - 1, 0)], 0, rows // 8 - 1, 0)
    seq = lambda c, place: (back(c), 0, 0, 0)
    seq5 = lambda c, place: (back(c), 0, 0, 0, 0)
    fact = lambda c, place: (0, back(c), 0, 0)

    def body(*refs):
        backward_kernel(heads, *refs)

    return pl.pallas_call(
        body,
        grid_spec=pltpu.PrefetchScalarGridSpec(
            num_scalar_prefetch=1,
            grid=(blocks,),
            in_specs=[
                pl.BlockSpec((1, group, rows, total), at),
                pl.BlockSpec((1, group, 8, total), before),
                pl.BlockSpec((group, 1, rows, 16), fact),
                pl.BlockSpec((group, 1, 8, rows), fact),
                whole(conv_rows.shape),
                whole(scal.shape),
                whole(gain.shape),
                pl.BlockSpec((1, group, rows, width), at),
                pl.BlockSpec((1, group, rows, width), seq),
                pl.BlockSpec((1, group, heads, rows, rows), seq5),
                pl.BlockSpec((1, group, rows, width), seq),
                pl.BlockSpec((1, group, heads, HD, HD), seq5),
            ],
            out_specs=[
                pl.BlockSpec((1, group, rows, total), at),
                whole((16, width)),
                whole((8, LANES)),
                whole((8, width)),
            ],
            scratch_shapes=[
                pltpu.VMEM((group, rows + 8, 3 * width), F32),
                pltpu.VMEM((group, rows + 8, 3 * width), F32),
                pltpu.VMEM((group, heads, HD, HD), F32),
            ],
        ),
        out_shape=[
            jax.ShapeDtypeStruct((blocks, group, rows, total), BF),
            jax.ShapeDtypeStruct((16, width), F32),
            jax.ShapeDtypeStruct((8, LANES), F32),
            jax.ShapeDtypeStruct((8, width), F32),
        ],
        compiler_params=pltpu.CompilerParams(**PARAMS),
        cost_estimate=pl.CostEstimate(
            flops=BACKWARD_COST * blocks * group * heads, bytes_accessed=12_000_000, transcendentals=0
        ),
        name="mixer_backward",
    )(place, raw, raw, aux, segrow, conv_rows, scal, gain, d_mixed, core, inverse, update, states)


def hop(values, bit, axis="head"):
    size = lax.axis_size(axis)
    return lax.ppermute(values, axis, [(i, i ^ bit) for i in range(size)])


def after(values, *earlier):
    kept = [item for group in earlier for item in (group if isinstance(group, list) else [group])]
    if not kept:
        return values
    return lax.optimization_barrier((values, *kept))[0]


def butterfly(values, axes):
    for axis in axes:
        bit = 1
        while bit < lax.axis_size(axis):
            values = values + hop(values, bit, axis)
            bit *= 2
    return values


def gather_near(values, *earlier):
    if earlier:
        values = after(values, *earlier)
    if lax.axis_size("head") != 4:
        return [lax.all_gather(values, "head", axis=0, tiled=True)]
    return [values, hop(values, 1), hop(values, 2)]


def gather_far(near, *earlier):
    if len(near) == 1:
        return []
    half = near[0].shape[0] // 2
    return [hop(after(near[2][:half], *earlier), 1), hop(after(near[1][half:], *earlier), 2)]


def block_parts(size, rows):
    if size != 4:
        return [[(0, r * rows, rows)] for r in range(size)]
    half = rows // 2
    return [[(0, 0, rows)], [(1, 0, rows)], [(2, 0, rows)], [(3, 0, half), (4, 0, half)]]


def joined(arrays):
    return arrays[0] if len(arrays) == 1 else jnp.concatenate(arrays, axis=0)


def scatter_plan(size, rows):
    half = rows // 2
    if size != 4:
        return [size * rows], {(r, h): (0, r * rows + h * half) for r in range(size) for h in (0, 1)}
    return [rows, rows, 2 * rows], {
        (1, 0): (0, 0), (3, 0): (0, half),
        (2, 1): (1, 0), (3, 1): (1, half),
        (0, 0): (2, 0), (0, 1): (2, half), (2, 0): (2, 2 * half), (1, 1): (2, 3 * half),
    }


def scatter_near(arrays, *earlier):
    if len(arrays) == 1:
        part = after(arrays[0], *earlier)
        return [lax.psum_scatter(part, "head", scatter_dimension=0, tiled=True)]
    to_x, to_y, keep = arrays
    return [hop(after(to_x, *earlier), 1), hop(after(to_y, *earlier), 2), keep]


def scatter_far(near):
    if len(near) == 1:
        return near[0].astype(F32)
    in_x, in_y, keep = near
    half = in_x.shape[0] // 2
    pass_y = (keep[2 * half : 3 * half].astype(F32) + in_x[half:].astype(F32)).astype(BF)
    pass_x = (keep[3 * half :].astype(F32) + in_y[half:].astype(F32)).astype(BF)
    last_y = hop(pass_y, 2).astype(F32)
    last_x = hop(pass_x, 1).astype(F32)
    near_sum = jnp.concatenate([in_x[:half], in_y[:half]], axis=0).astype(F32)
    last = jnp.concatenate([last_y, last_x], axis=0)
    return keep[: 2 * half].astype(F32) + near_sum + last


def arranged(product, size):
    rows = product.shape[0] // size
    counts, where = scatter_plan(size, rows)
    half = rows // 2
    pieces = [[None] * (count // half) for count in counts]
    for (block, h), (index, at) in where.items():
        start = block * rows + h * half
        pieces[index][at // half] = product[start : start + half]
    return [jnp.concatenate(item, axis=0).astype(BF) for item in pieces]


def ffn_kernel(turns, rows, parts, n_pieces, where, n_out, aliased, *refs):
    mids, cots = refs[:n_pieces], refs[n_pieces : 2 * n_pieces]
    wg_ref, wu_ref, wd_ref = refs[2 * n_pieces : 2 * n_pieces + 3]
    refs = refs[2 * n_pieces + 3 + (2 * n_out if aliased else 0) :]
    act_ref, dg_ref, du_ref, xo_ref, co_ref = refs[:5]
    gm_refs, ff_refs = refs[5 : 5 + n_out], refs[5 + n_out : 5 + 2 * n_out]
    wg, wu, wd, xbuf, cbuf, gm_buf, ff_buf, w_sem, x_sem, c_sem, o_sem = refs[5 + 2 * n_out :]
    step = pl.program_id(0)
    half = rows // 2
    steps = len(turns)

    def loads(turn):
        slot = turn % 2
        found = []
        for arrays, buf, sem in ((mids, xbuf, x_sem), (cots, cbuf, c_sem)):
            place = 0
            for k, (index, at, count) in enumerate(parts[turns[turn]]):
                found.append(
                    pltpu.make_async_copy(
                        arrays[index].at[at : at + count],
                        buf.at[slot, place : place + count],
                        sem.at[slot, k],
                    )
                )
                place += count
        return found

    def stores(turn):
        slot = turn % 2
        found = []
        for k, (buf, outs) in enumerate(((gm_buf, gm_refs), (ff_buf, ff_refs))):
            for h in (0, 1):
                index, at = where[(turns[turn], h)]
                found.append(
                    pltpu.make_async_copy(
                        buf.at[slot, h * half : (h + 1) * half],
                        outs[index].at[at : at + half],
                        o_sem.at[slot, 2 * k + h],
                    )
                )
        return found

    weights = [
        pltpu.make_async_copy(src, dst, w_sem.at[k])
        for k, (src, dst) in enumerate(((wg_ref, wg), (wu_ref, wu), (wd_ref, wd)))
    ]

    @pl.when(step == 0)
    def _():
        for copy in loads(0):
            copy.start()
        for copy in weights:
            copy.start()

    for turn in range(steps):
        @pl.when(step == turn)
        def _(turn=turn):
            if turn + 1 < steps:
                for copy in loads(turn + 1):
                    copy.start()
            for copy in loads(turn):
                copy.wait()
            if turn >= 2:
                for copy in stores(turn - 2):
                    copy.wait()

    slot = lax.rem(step, 2)

    @pl.when(step == 0)
    def _():
        weights[0].wait()

    x = xbuf[slot]
    gate = jnp.dot(x, wg[...], preferred_element_type=F32)

    @pl.when(step == 0)
    def _():
        weights[1].wait()

    upward = jnp.dot(x, wu[...], preferred_element_type=F32)

    @pl.when(step == 0)
    def _():
        weights[2].wait()

    cot = cbuf[slot]
    d_act = jnp.dot(cot, wd[...], preferred_element_type=F32)
    open_ = sigmoid(gate)
    silu = gate * open_
    act = (silu * upward).astype(BF)
    d_gate = (d_act * upward * open_ * (1.0 + gate * (1.0 - open_))).astype(BF)
    d_up = (d_act * silu).astype(BF)
    act_ref[0] = act
    dg_ref[0] = d_gate
    du_ref[0] = d_up
    xo_ref[0] = x
    co_ref[0] = cot
    gm_buf[slot] = (mm_nt(d_gate, wg[...]) + mm_nt(d_up, wu[...])).astype(BF)
    ff_buf[slot] = mm_nt(act, wd[...]).astype(BF)
    for turn in range(steps):
        @pl.when(step == turn)
        def _(turn=turn):
            for copy in stores(turn):
                copy.start()
            if turn == steps - 1:
                for earlier in range(max(0, steps - 2), steps):
                    for copy in stores(earlier):
                        copy.wait()


def ffn_stage(turns, mids, cots, weights, size, filled=None):
    width, hidden = weights[0].shape
    rows = mids[0].shape[0] if size == 4 else mids[0].shape[0] // size
    parts = block_parts(size, rows)
    counts, where = scatter_plan(size, rows)
    aliased = filled is not None
    filled = list(filled) if aliased else []

    def body(*refs):
        ffn_kernel(turns, rows, parts, len(mids), where, len(counts), aliased, *refs)

    anywhere = pl.BlockSpec(memory_space=pl.ANY)
    by_block = lambda last: pl.BlockSpec((1, rows, last), lambda i: (i, 0, 0))
    steps = len(turns)
    first = 2 * len(mids) + 3
    out = pl.pallas_call(
        body,
        grid=(steps,),
        in_specs=[anywhere] * (first + len(filled)),
        out_specs=[by_block(hidden)] * 3 + [by_block(width)] * 2 + [anywhere] * (2 * len(counts)),
        out_shape=[jax.ShapeDtypeStruct((steps, rows, hidden), BF)] * 3
        + [jax.ShapeDtypeStruct((steps, rows, width), BF)] * 2
        + [jax.ShapeDtypeStruct((c, width), BF) for c in counts] * 2,
        input_output_aliases={first + k: 5 + k for k in range(len(filled))},
        scratch_shapes=[
            pltpu.VMEM((width, hidden), BF),
            pltpu.VMEM((width, hidden), BF),
            pltpu.VMEM((width, hidden), BF),
            pltpu.VMEM((2, rows, width), BF),
            pltpu.VMEM((2, rows, width), BF),
            pltpu.VMEM((2, rows, width), BF),
            pltpu.VMEM((2, rows, width), BF),
            pltpu.SemaphoreType.DMA((3,)),
            pltpu.SemaphoreType.DMA((2, 2)),
            pltpu.SemaphoreType.DMA((2, 2)),
            pltpu.SemaphoreType.DMA((2, 4)),
        ],
        compiler_params=pltpu.CompilerParams(**PARAMS),
        cost_estimate=pl.CostEstimate(
            flops=steps * rows * width * hidden * 20, bytes_accessed=30_000_000, transcendentals=0
        ),
        name="ffn_stage",
    )(*mids, *cots, *weights, *filled)
    flat = [array.reshape(steps * rows, array.shape[-1]) for array in out[:5]]
    return flat, list(out[5:])


def wgrad_kernel(count, *refs):
    lefts, rights, out_ref = refs[:count], refs[count : 2 * count], refs[2 * count]
    total = mm_tn(lefts[0][...], rights[0][...])
    for left, right in zip(lefts[1:], rights[1:]):
        total = total + mm_tn(left[...], right[...])
    out_ref[...] = total.astype(BF)


def weight_gradient(lefts, rights):
    depth, wide = lefts[0].shape
    columns = rights[0].shape[1]
    tile = 512 if wide % 512 == 0 else wide
    count = len(lefts)
    return pl.pallas_call(
        lambda *refs: wgrad_kernel(count, *refs),
        grid=(wide // tile,),
        in_specs=[pl.BlockSpec((depth, tile), lambda i: (0, i))] * count
        + [pl.BlockSpec((depth, columns), lambda i: (0, 0))] * count,
        out_specs=pl.BlockSpec((tile, columns), lambda i: (i, 0)),
        out_shape=jax.ShapeDtypeStruct((wide, columns), BF),
        compiler_params=pltpu.CompilerParams(**PARAMS),
        cost_estimate=pl.CostEstimate(
            flops=3 * count * depth * wide * columns, bytes_accessed=20_000_000, transcendentals=0
        ),
        name="weight_gradient",
    )(*lefts, *rights)


def block_places(size):
    base = lax.iota(jnp.int32, size)
    if size != 4:
        return base
    return base ^ lax.axis_index("head").astype(jnp.int32)


def contract_rows(left, right):
    return lax.dot_general(left, right, (((0,), (0,)), ((), ())), preferred_element_type=F32)


def contract_cols(left, right):
    return lax.dot_general(left, right, (((1,), (1,)), ((), ())), preferred_element_type=F32)


def times(left, right):
    return jnp.dot(left, right, preferred_element_type=F32)


def sequence_facts(doc_lengths, blocks, rows):
    span = blocks * rows
    ends = jnp.cumsum(doc_lengths, axis=-1)
    places = lax.iota(jnp.int32, span)
    segment = jnp.sum((places[None, :, None] >= ends[:, None, :]).astype(jnp.int32), axis=-1)
    columns = [segment]
    for j in range(1, 4):
        columns.append(
            (jnp.pad(segment, ((0, 0), (j, 0)), constant_values=-1)[:, :-j] == segment)
        )
    by_chunk = segment.reshape(-1, blocks, rows)
    prior = jnp.pad(by_chunk[:, :-1, -1], ((0, 0), (1, 0)), constant_values=-1)
    columns.append((by_chunk == prior[:, :, None]).reshape(segment.shape))
    columns.append((by_chunk == by_chunk[:, :, -1:]).reshape(segment.shape))
    columns += [jnp.zeros_like(segment)] * 2
    for j in range(1, 4):
        columns.append(
            (jnp.pad(segment, ((0, 0), (0, j)), constant_values=-1)[:, j:] == segment)
        )
    columns += [jnp.zeros_like(segment)] * (16 - len(columns))
    aux = jnp.stack([item.astype(F32) for item in columns], axis=-1)
    aux = aux.reshape(-1, blocks, rows, 16)
    lines = jnp.broadcast_to(by_chunk.astype(F32)[:, :, None, :], by_chunk.shape[:2] + (8, rows))
    return aux, lines


def on_device(
    tokens, cotangent, token_counts, doc_lengths, norm_in, w_query, w_key, w_value, w_outgate,
    w_decay, w_beta, conv_weight, decay_log, dt_bias, gain_out, w_out, norm_mid, w_gate, w_up,
    w_down,
):
    micro_count, rows, width = tokens.shape
    blocks = lax.axis_size("head")
    group = micro_count // 2
    own_rows = group * rows
    span = own_rows * blocks
    heads = decay_log.shape[0]
    own = heads * HD
    groups = range(micro_count // group)
    my_places = lax.axis_index("head") * rows + lax.iota(jnp.int32, rows)
    live = (my_places[None, :] < token_counts[:, :1]).astype(F32)[:, :, None]
    place = block_places(blocks)
    aux, lines = sequence_facts(doc_lengths[:, 0], blocks, rows)
    conv_rows = jnp.pad(conv_weight.reshape(12, own), ((0, 4), (0, 0)))
    scal = jnp.zeros((8, LANES), F32)
    scal = scal.at[0, :heads].set(-jnp.exp(decay_log)).at[1, :heads].set(dt_bias)
    gain_row = jnp.broadcast_to(gain_out[None], (8, own))
    ffn_gate = lax.all_gather(w_gate, "dp", axis=0, tiled=True)
    ffn_up = lax.all_gather(w_up, "dp", axis=0, tiled=True)
    ffn_down = lax.all_gather(w_down, "dp", axis=0, tiled=True)

    def of_group(array, i):
        return array[i * group : (i + 1) * group]

    inputs, grads, lives, pulls_in, normed_in = [], [], [], [], []
    for i in groups:
        x = of_group(tokens, i).reshape(own_rows, width).astype(F32)
        normed, pull = jax.vjp(norm_rows, x, norm_in)
        inputs.append(x)
        pulls_in.append(pull)
        normed_in.append(normed.astype(BF))
        grads.append((of_group(cotangent, i).astype(F32) * of_group(live, i)).reshape(own_rows, width))
    cots = [item.astype(BF) for item in grads]
    in_a1 = gather_near(normed_in[0])
    w_in = jnp.concatenate(
        [after(w_query, in_a1), w_key, w_value, w_outgate, w_decay, w_beta,
         jnp.zeros((width, LANES - 2 * heads), BF)], axis=1
    )

    def project(full):
        return times(full, w_in).reshape(blocks, group, rows, 4 * own + LANES)

    def mix(raw, i):
        mixed, *saved = mixer_forward(
            place, raw, of_group(aux, i), of_group(lines, i), conv_rows, scal, gain_row
        )
        return mixed.reshape(span, own), saved

    def out_of(mixed):
        return arranged(times(mixed, w_out), blocks)

    def middle(i, attn):
        resid = inputs[i] + attn
        normed, pull = jax.vjp(norm_rows, resid, norm_mid)
        return resid, pull, normed.astype(BF)

    in_a2 = gather_far(in_a1)
    in_b1 = gather_near(normed_in[1], in_a2)
    full_a = joined(in_a1 + in_a2)
    raw_a = project(full_a)
    in_b2 = gather_far(in_b1)
    mixed_a, saved_a = mix(raw_a, 0)
    attn_a = out_of(after(mixed_a, in_b1))
    full_b = joined(in_b1 + in_b2)
    at_a1 = scatter_near(attn_a)
    raw_b = project(after(full_b, attn_a))
    cot_a1 = gather_near(cots[0], at_a1)
    mixed_b, saved_b = mix(after(raw_b, at_a1), 1)
    sum_a = scatter_far(at_a1)
    cot_a2 = gather_far(cot_a1)
    attn_b = out_of(after(mixed_b, sum_a, cot_a1))
    resid_a, pull_a, mid_a = middle(0, sum_a)
    mid_a1 = gather_near(mid_a)
    at_b1 = scatter_near(attn_b, cot_a1)
    mid_a2 = gather_far(mid_a1)
    sum_b = scatter_far(at_b1)
    resid_b, pull_b, mid_b = middle(1, sum_b)
    mid_b1 = gather_near(mid_b, mid_a2, cot_a2)
    cot_b1 = gather_near(cots[1], mid_a2, cot_a2)

    ffn_weights = [ffn_gate, ffn_up, ffn_down]
    first_turns = (1, 3) if blocks == 4 else tuple(range(blocks // 2))
    last_turns = tuple(r for r in range(blocks) if r not in first_turns)
    outs = len(scatter_plan(blocks, own_rows)[0])
    kept_a, begun = ffn_stage(first_turns, mid_a1 + mid_a2, cot_a1 + cot_a2, ffn_weights, blocks)
    mid_b2 = gather_far(mid_b1)
    cot_b2 = gather_far(cot_b1)
    begun = [after(begun[0], mid_b1)] + begun[1:]
    kept_a2, out_a = ffn_stage(
        last_turns, mid_a1 + mid_a2, cot_a1 + cot_a2, ffn_weights, blocks, begun
    )
    gm_a1 = scatter_near(out_a[:outs])
    near_b = mid_b1 + mid_b2
    near_b[0] = after(near_b[0], out_a[0])
    kept_b, begun = ffn_stage(first_turns, near_b, cot_b1 + cot_b2, ffn_weights, blocks)
    begun = [after(begun[0], gm_a1)] + begun[1:]
    kept_b2, out_b = ffn_stage(last_turns, near_b, cot_b1 + cot_b2, ffn_weights, blocks, begun)
    kept = [kept_a, kept_a2, kept_b, kept_b2]
    acts, gates, ups, mids, cot_all = [[item[k] for item in kept] for k in range(5)]

    def share(term):
        return lax.psum_scatter(term, "dp", scatter_dimension=0, tiled=True).astype(F32)

    def resid_back(i, pull, d_mid):
        d_resid, d_norm = pull(d_mid)
        d_resid = grads[i] + d_resid
        return d_resid, d_norm, d_resid.astype(BF)

    d_mid_a = scatter_far(gm_a1)
    gm_b1 = scatter_near(out_b[:outs], d_mid_a)
    d_resid_a, gain_mid_a, low_a = resid_back(0, pull_a, d_mid_a)
    gates[0] = after(gates[0], low_a)
    rg_a1 = gather_near(low_a)
    term_gate = weight_gradient(mids, gates)
    grad_gate = share(term_gate)
    rg_a2 = gather_far(rg_a1)
    d_mid_b = scatter_far(gm_b1)
    ups[0] = after(ups[0], term_gate, rg_a1, gm_b1)
    term_up = weight_gradient(mids, ups)
    grad_up = share(term_up)
    d_resid_b, gain_mid_b, low_b = resid_back(1, pull_b, d_mid_b)
    rg_b1 = gather_near(low_b)
    rg_b2 = gather_far(rg_b1)
    full_ra = joined(rg_a1 + rg_a2)
    full_rb = joined(rg_b1 + rg_b2)

    def back(i, full, raw, saved):
        d_mixed = contract_cols(full, w_out).reshape(blocks, group, rows, own)
        return mixer_backward(
            place, raw, of_group(aux, i), of_group(lines, i), conv_rows, scal, gain_row,
            d_mixed, saved,
        )

    def in_back(d_raw):
        return arranged(contract_cols(d_raw, w_in), blocks)

    d_raw_a, *sums_a = back(0, after(full_ra, term_up, low_b), raw_a, saved_a)
    d_raw_a = d_raw_a.reshape(span, 4 * own + LANES)
    acts[0] = after(acts[0], d_raw_a, rg_b1)
    term_down = weight_gradient(cot_all, acts)
    grad_down = share(term_down)
    d_in_a = in_back(after(d_raw_a, term_down, rg_b2))
    gi_a1 = scatter_near(d_in_a)
    ff_a1 = scatter_near(out_a[outs:], d_in_a)
    term_out = weight_gradient([after(full_ra, d_in_a), full_rb], [mixed_a, mixed_b])
    grad_out = share(term_out).T
    d_raw_b, *sums_b = back(1, after(full_rb, term_out, grad_gate), raw_b, saved_b)
    d_raw_b = d_raw_b.reshape(span, 4 * own + LANES)
    d_norm_a = scatter_far(gi_a1)
    ffn_a = scatter_far(ff_a1)
    ff_b1 = scatter_near(out_b[outs:], d_norm_a, ffn_a)
    d_in_b = in_back(after(d_raw_b, d_norm_a, ffn_a, grad_up))
    gi_b1 = scatter_near(d_in_b)
    term_in = weight_gradient([full_a, full_b], [d_raw_a, after(d_raw_b, d_in_b)])
    grad_in = share(term_in)
    ffn_b = scatter_far(ff_b1)
    d_norm_b = scatter_far(gi_b1)

    results, input_grads = [], []
    gain_in = jnp.zeros_like(norm_in)
    for i, (resid, ffn, d_resid, d_norm) in enumerate(
        ((resid_a, ffn_a, d_resid_a, d_norm_a), (resid_b, ffn_b, d_resid_b, d_norm_b))
    ):
        results.append((resid + ffn).astype(BF).reshape(group, rows, width))
        d_inputs, d_gain = pulls_in[i](d_norm)
        input_grads.append((d_inputs + d_resid).astype(BF).reshape(group, rows, width))
        gain_in = gain_in + d_gain
    gain_mid = gain_mid_a + gain_mid_b
    small_sums = [left + right for left, right in zip(sums_a, sums_b)]
    small_sums[0] = after(small_sums[0], d_in_b)
    wide = jnp.concatenate([small_sums[0][:12], small_sums[2][:4]], axis=0)
    wide = butterfly(wide, ("dp",))
    narrow = butterfly(small_sums[1], ("dp",))
    gains = butterfly(jnp.stack([gain_in, gain_mid]), ("dp", "head"))
    return (
        jnp.concatenate(results, axis=0),
        jnp.concatenate(input_grads, axis=0),
        gains[0],
        grad_in[:, :own],
        grad_in[:, own : 2 * own],
        grad_in[:, 2 * own : 3 * own],
        grad_in[:, 3 * own : 4 * own],
        grad_in[:, 4 * own : 4 * own + heads],
        grad_in[:, 4 * own + heads : 4 * own + 2 * heads],
        wide[:12].reshape(conv_weight.shape),
        narrow[0, :heads],
        narrow[1, :heads],
        wide[12],
        grad_out,
        gains[1],
        grad_gate,
        grad_up,
        grad_down,
    )


def solution(mesh):
    return jax.shard_map(
        on_device,
        mesh=mesh,
        in_specs=(
            P(None, ("dp", "head"), None),
            P(None, ("dp", "head"), None),
            P(None, "dp"),
            P(None, "dp", None),
            P(),
            P(None, "head"),
            P(None, "head"),
            P(None, "head"),
            P(None, "head"),
            P(None, "head"),
            P(None, "head"),
            P(None, None, "head"),
            P("head"),
            P("head"),
            P("head"),
            P("head", None),
            P(),
            P("dp", "head"),
            P("dp", "head"),
            P("dp", "head"),
        ),
        out_specs=(
            P(None, ("dp", "head"), None),
            P(None, ("dp", "head"), None),
            P(),
            P("dp", "head"),
            P("dp", "head"),
            P("dp", "head"),
            P("dp", "head"),
            P("dp", "head"),
            P("dp", "head"),
            P(None, None, "head"),
            P("head"),
            P("head"),
            P("head"),
            P("head", "dp"),
            P(),
            P("dp", "head"),
            P("dp", "head"),
            P("dp", "head"),
        ),
        check_vma=False,
    )
```

```python
import jax
import jax.numpy as jnp
from jax import lax
from jax.experimental import pallas as pl
from jax.experimental.pallas import tpu as pltpu
from jax.sharding import PartitionSpec as P

HD = 128
LANES = 128
SCALE = HD ** (-0.5)
BF = jnp.bfloat16
F32 = jnp.float32
FORWARD_COST = 735_000_000
BACKWARD_COST = 1_650_000_000


def norm_rows(values, gain):
    return values * lax.rsqrt(jnp.mean(values * values, axis=-1, keepdims=True) + 1e-05) * gain


def swiglu(gate, upward):
    return jax.nn.silu(gate) * upward


def mm(left, right):
    return jnp.dot(left.astype(BF), right.astype(BF), preferred_element_type=F32)


def mm_nt(left, right):
    return lax.dot_general(
        left.astype(BF), right.astype(BF), (((1,), (1,)), ((), ())), preferred_element_type=F32
    )


def mm_tn(left, right):
    return lax.dot_general(
        left.astype(BF), right.astype(BF), (((0,), (0,)), ((), ())), preferred_element_type=F32
    )


def mm_exact(left, right):
    return jnp.dot(left, right, preferred_element_type=F32, precision=lax.Precision.HIGHEST)


def sigmoid(values):
    return 1.0 / (1.0 + jnp.exp(-values))


def softplus(values):
    return jnp.maximum(values, 0.0) + jnp.log1p(jnp.exp(-jnp.abs(values)))


def chunk_masks(rows):
    row_ids = lax.broadcasted_iota(jnp.int32, (rows, rows), 0)
    col_ids = lax.broadcasted_iota(jnp.int32, (rows, rows), 1)
    return row_ids, col_ids


def chunk_gates(small, scal_ref, aux, tri):
    rows = small.shape[0]
    log_alpha = scal_ref[0:1, :] * softplus(small + scal_ref[1:2, :])
    beta = sigmoid(small)
    decay_sum = mm_exact(tri, log_alpha)
    last = decay_sum[rows - 1 : rows, :]
    carried = aux[:, 4:5]
    growth = jnp.exp(decay_sum) * carried
    tail = jnp.exp(last - decay_sum) * aux[:, 5:6]
    keep = jnp.exp(last) * carried[rows - 1 : rows, :]
    return log_alpha, beta, decay_sum, growth, tail, keep


def spread_out(columns, index):
    return jnp.broadcast_to(columns[:, index : index + 1], (columns.shape[0], HD))


def conv_of(ext_ref, conv_ref, masks, m, index, head, rows, width):
    lanes = slice(index * width + head * HD, index * width + (head + 1) * HD)
    own = slice(head * HD, (head + 1) * HD)
    taps = [ext_ref[m, 8 : 8 + rows, lanes]]
    for j in range(1, 4):
        taps.append(ext_ref[m, 8 - j : 8 - j + rows, lanes] * masks[j - 1])
    total = taps[0] * conv_ref[4 * index : 4 * index + 1, own]
    for j in range(1, 4):
        total = total + taps[j] * conv_ref[4 * index + j : 4 * index + j + 1, own]
    return total, taps


def invert_unit_lower(powers, row_ids, col_ids):
    rows = row_ids.shape[0]
    eye = (row_ids == col_ids).astype(F32)
    pair = (row_ids // 2) == (col_ids // 2)
    inverses = [eye - jnp.where(pair, power, 0.0) for power in powers]
    half = 2
    while half < rows:
        joint = ((row_ids // (2 * half)) == (col_ids // (2 * half))) & (
            (row_ids // half) != (col_ids // half)
        )
        lows = [inverse.astype(BF) for inverse in inverses]
        firsts = [mm(low, jnp.where(joint, power, 0.0)) for low, power in zip(lows, powers)]
        inverses = [
            inverse - mm(first, low) for inverse, first, low in zip(inverses, firsts, lows)
        ]
        half *= 2
    return [inverse.astype(BF) for inverse in inverses]


def forward_kernel(
    heads, place_ref, raw_ref, aux_ref, segrow_ref, conv_ref, scal_ref, gain_ref,
    mixed_ref, core_ref, inv_ref, upd_ref, st_ref, ext_ref, state_ref,
):
    step = pl.program_id(0)
    group, rows = raw_ref.shape[1:3]
    width = heads * HD
    row_ids, col_ids = chunk_masks(rows)
    tri = (row_ids >= col_ids).astype(F32)
    strict = row_ids > col_ids

    @pl.when(step == 0)
    def _():
        ext_ref[:, 0:8, :] = jnp.zeros((group, 8, 3 * width), F32)
        state_ref[...] = jnp.zeros_like(state_ref)

    ext_ref[:, 8 : 8 + rows, :] = raw_ref[0, :, :, 0 : 3 * width]
    chains = [(m, h) for m in range(group) for h in range(heads)]
    stacked, values, powers, outs, betas, growths, tails, keeps = [], [], [], [], [], [], [], []
    for m in range(group):
        aux = aux_ref[m, 0]
        small = raw_ref[0, m, :, 4 * width : 4 * width + LANES]
        _, beta, decay_sum, growth, tail, keep = chunk_gates(small, scal_ref, aux, tri)
        masks = [spread_out(aux, j) for j in range(1, 4)]
        decay_rows = decay_sum.T
        below = (row_ids >= col_ids) & (aux[:, 0:1] == segrow_ref[m, 0, 0:1, :])
        for head in range(heads):
            query, _ = conv_of(ext_ref, conv_ref, masks, m, 0, head, rows, width)
            query = query * sigmoid(query)
            query = query * (
                lax.rsqrt(jnp.sum(query * query, axis=-1, keepdims=True) + 1e-06) * SCALE
            )
            key, _ = conv_of(ext_ref, conv_ref, masks, m, 1, head, rows, width)
            key = key * sigmoid(key)
            key = key * lax.rsqrt(jnp.sum(key * key, axis=-1, keepdims=True) + 1e-06)
            value, _ = conv_of(ext_ref, conv_ref, masks, m, 2, head, rows, width)
            value = value * sigmoid(value)
            b_col = spread_out(beta, heads + head)
            spread = decay_sum[:, head : head + 1] - decay_rows[head : head + 1, :]
            inside = jnp.exp(jnp.where(below, spread, -1e30))
            both = jnp.concatenate([key, query], axis=0).astype(BF)
            dots = mm_nt(both, both[:rows])
            stacked.append(both)
            values.append(value)
            powers.append(jnp.where(strict, b_col[:, :rows] * dots[:rows] * inside, 0.0))
            outs.append((dots[rows:] * inside).astype(BF))
            betas.append(b_col)
            growths.append(spread_out(growth, head))
            tails.append(spread_out(tail, head))
            keeps.append(keep[:, head : head + 1])
    inverses = invert_unit_lower(powers, row_ids, col_ids)
    states = [state_ref[m, h] for m, h in chains]
    lows = [state.astype(BF) for state in states]
    applied = [mm(both, low) for both, low in zip(stacked, lows)]
    updates = []
    for i, (m, h) in enumerate(chains):
        st_ref[0, m, h] = lows[i]
        inv_ref[0, m, h] = inverses[i]
        rest = betas[i] * (values[i] - growths[i] * applied[i][:rows])
        updates.append(mm(inverses[i], rest).astype(BF))
    for i, (m, h) in enumerate(chains):
        lanes = slice(h * HD, (h + 1) * HD)
        upd_ref[0, m, :, lanes] = updates[i]
        state_ref[m, h] = keeps[i] * states[i] + mm_tn(
            stacked[i][:rows].astype(F32) * tails[i], updates[i]
        )
        core = growths[i] * applied[i][rows:] + mm(outs[i], updates[i])
        core_ref[0, m, :, lanes] = core
        outgate = raw_ref[0, m, :, 3 * width + h * HD : 3 * width + (h + 1) * HD]
        normed = core * lax.rsqrt(jnp.mean(core * core, axis=-1, keepdims=True) + 1e-05)
        mixed_ref[0, m, :, lanes] = (
            normed * gain_ref[0:1, lanes] * (outgate * sigmoid(outgate))
        ).astype(BF)
    ext_ref[:, 0:8, :] = ext_ref[:, rows : rows + 8, :]


def backward_kernel(
    heads, place_ref, raw_ref, prev_ref, aux_ref, segrow_ref, conv_ref, scal_ref, gain_ref,
    dmix_ref, core_ref, inv_ref, upd_ref, st_ref,
    draw_ref, dconv_ref, dscal_ref, dgain_ref, ext_ref, dext_ref, dstate_ref,
):
    step = pl.program_id(0)
    group, rows = raw_ref.shape[1:3]
    width = heads * HD

    @pl.when(step == 0)
    def _():
        dext_ref[:, rows : rows + 8, :] = jnp.zeros((group, 8, 3 * width), F32)
        dstate_ref[...] = jnp.zeros_like(dstate_ref)
        dconv_ref[...] = jnp.zeros_like(dconv_ref)
        dscal_ref[...] = jnp.zeros_like(dscal_ref)
        dgain_ref[...] = jnp.zeros_like(dgain_ref)

    @pl.when(step > 0)
    def _():
        dext_ref[:, rows : rows + 8, :] = dext_ref[:, 0:8, :]

    ext_ref[:, 0:8, :] = prev_ref[0, :, :, 0 : 3 * width]
    ext_ref[:, 8 : 8 + rows, :] = raw_ref[0, :, :, 0 : 3 * width]
    row_ids, col_ids = chunk_masks(rows)
    tri = (row_ids >= col_ids).astype(F32)
    upper = (row_ids <= col_ids).astype(F32)
    strict = row_ids > col_ids
    lane_ids = lax.broadcasted_iota(jnp.int32, (rows, LANES), 1)
    line_ids = lax.broadcasted_iota(jnp.int32, (LANES, rows), 0)
    last_row = lax.broadcasted_iota(jnp.int32, (rows, 1), 0) == rows - 1

    def conv_back(m, index, head, later, taps, d_conv):
        lanes = slice(index * width + head * HD, index * width + (head + 1) * HD)
        own = slice(head * HD, (head + 1) * HD)
        dext_ref[m, 0:rows, lanes] = d_conv
        total = d_conv * conv_ref[4 * index : 4 * index + 1, own]
        for j in range(4):
            line = 4 * index + j
            dconv_ref[8 * line : 8 * line + 8, own] += jnp.sum(
                (d_conv * taps[j]).reshape(rows // 8, 8, HD), axis=0
            )
        for j in range(1, 4):
            line = slice(4 * index + j, 4 * index + j + 1)
            total = total + dext_ref[m, j : j + rows, lanes] * conv_ref[line, own] * later[j - 1]
        draw_ref[0, m, :, lanes] = total.astype(BF)

    for m in range(group):
        aux = aux_ref[m, 0]
        small = raw_ref[0, m, :, 4 * width : 4 * width + LANES]
        log_alpha, beta, decay_sum, growth, tail, keep = chunk_gates(small, scal_ref, aux, tri)
        masks = [spread_out(aux, j) for j in range(1, 4)]
        later = [spread_out(aux, 7 + j) for j in range(1, 4)]
        decay_rows = decay_sum.T
        below = (row_ids >= col_ids) & (aux[:, 0:1] == segrow_ref[m, 0, 0:1, :])
        d_decay = jnp.zeros((rows, LANES), F32)
        d_beta = jnp.zeros((rows, LANES), F32)
        d_decay_lines = jnp.zeros((LANES, rows), F32)
        everyone = range(heads)
        own_lanes = [slice(h * HD, (h + 1) * HD) for h in everyone]
        b_cols = [spread_out(beta, heads + h) for h in everyone]
        g_cols = [spread_out(growth, h) for h in everyone]
        t_cols = [spread_out(tail, h) for h in everyone]
        keeps = [keep[:, h : h + 1] for h in everyone]
        d_cores, queries, keys, values = [], [], [], []
        for h in everyone:
            lanes = own_lanes[h]
            gate_lanes = slice(3 * width + h * HD, 3 * width + (h + 1) * HD)
            outgate = raw_ref[0, m, :, gate_lanes]
            gate = sigmoid(outgate)
            core = core_ref[0, m, :, lanes]
            inv_norm = lax.rsqrt(jnp.mean(core * core, axis=-1, keepdims=True) + 1e-05)
            normed = core * inv_norm
            d_mixed = dmix_ref[0, m, :, lanes].astype(F32)
            gain = gain_ref[0:1, lanes]
            d_silu = d_mixed * (outgate * gate)
            dgain_ref[0:1, lanes] += jnp.sum(d_silu * normed, axis=0, keepdims=True)
            draw_ref[0, m, :, gate_lanes] = (
                d_mixed * normed * gain * (gate * (1.0 + outgate * (1.0 - gate)))
            ).astype(BF)
            d_normed = d_silu * gain
            d_cores.append(
                (inv_norm * (d_normed - normed * jnp.mean(d_normed * normed, axis=-1, keepdims=True))).astype(BF)
            )
            parts = []
            for index in range(3):
                conv, taps = conv_of(ext_ref, conv_ref, masks, m, index, h, rows, width)
                gate = sigmoid(conv)
                act = conv * gate
                slope = gate * (1.0 + conv * (1.0 - gate))
                if index == 2:
                    parts.append((act, slope, taps))
                else:
                    root = lax.rsqrt(jnp.sum(act * act, axis=-1, keepdims=True) + 1e-06)
                    parts.append((act * root, slope * root, taps))
            queries.append(parts[0])
            keys.append(parts[1])
            values.append(parts[2])
        insides = [
            jnp.exp(jnp.where(below, decay_sum[:, h : h + 1] - decay_rows[h : h + 1, :], -1e30))
            for h in everyone
        ]
        key_lows = [keys[h][0].astype(BF) for h in everyone]
        query_lows = [(queries[h][0] * SCALE).astype(BF) for h in everyone]
        dots = [
            mm_nt(jnp.concatenate([key_lows[h], query_lows[h]], axis=0), key_lows[h])
            for h in everyone
        ]
        updates = [upd_ref[0, m, :, own_lanes[h]] for h in everyone]
        states = [st_ref[0, m, h] for h in everyone]
        d_states = [dstate_ref[m, h] for h in everyone]
        d_state_lows = [item.astype(BF) for item in d_states]
        outs = [dots[h][rows:] * insides[h] for h in everyone]
        d_updates = [
            mm_tn(outs[h], d_cores[h]) + mm(keys[h][0] * t_cols[h], d_state_lows[h])
            for h in everyone
        ]
        d_rests = [mm_tn(inv_ref[0, m, h], d_updates[h]) for h in everyone]
        pairs = [
            jnp.concatenate([d_cores[h], d_rests[h].astype(BF)], axis=0) for h in everyone
        ]
        boths = [mm_nt(pairs[h], updates[h]) for h in everyone]
        sides = [mm_nt(pairs[h], states[h]) for h in everyone]
        d_tail_keys = [mm_nt(updates[h], d_state_lows[h]) for h in everyone]
        for h in everyone:
            key, query = keys[h][0], queries[h][0]
            d_weights, d_power = boths[h][:rows], -boths[h][rows:]
            core_state, rest_state = sides[h][:rows], sides[h][rows:]
            key_dots = dots[h][:rows]
            d_query_dots = d_weights * insides[h]
            power_in = jnp.where(strict, d_power * insides[h], 0.0)
            d_key_dots = power_in * b_cols[h][:, :rows]
            reach = d_weights * outs[h] + d_key_dots * key_dots
            key_rest = jnp.sum(key * rest_state, axis=-1, keepdims=True)
            d_beta_col = (
                jnp.sum(power_in * key_dots, axis=-1, keepdims=True)
                + jnp.sum(d_rests[h] * values[h][0], axis=-1, keepdims=True)
                - growth[:, h : h + 1] * key_rest
            )
            d_growth = SCALE * jnp.sum(query * core_state, axis=-1, keepdims=True) - beta[:, heads + h : heads + h + 1] * key_rest
            tail_part = tail[:, h : h + 1] * jnp.sum(d_tail_keys[h] * key, axis=-1, keepdims=True)
            last_part = jnp.sum(tail_part, axis=0, keepdims=True) + keeps[h] * jnp.sum(
                jnp.sum(d_states[h] * states[h].astype(F32), axis=0, keepdims=True),
                axis=-1,
                keepdims=True,
            )
            d_sum_col = (
                jnp.sum(reach, axis=-1, keepdims=True)
                + growth[:, h : h + 1] * d_growth
                - tail_part
                + jnp.where(last_row, last_part, 0.0)
            )
            d_decay = jnp.where(lane_ids == h, d_sum_col, d_decay)
            d_beta = jnp.where(lane_ids == heads + h, d_beta_col, d_beta)
            d_decay_lines = jnp.where(
                line_ids == h, jnp.sum(reach, axis=0, keepdims=True), d_decay_lines
            )
            scale_rest = -(b_cols[h] * g_cols[h])
            dot_grads = jnp.concatenate([d_key_dots, d_query_dots], axis=0).astype(BF)
            by_key = mm(dot_grads, key_lows[h])
            d_query = (g_cols[h] * core_state + by_key[rows:]) * SCALE
            d_key = (
                scale_rest * rest_state
                + t_cols[h] * d_tail_keys[h]
                + by_key[:rows]
                + mm_tn(dot_grads, jnp.concatenate([key_lows[h], query_lows[h]], axis=0))
            )
            dstate_ref[m, h] = keeps[h] * d_states[h] + mm_tn(
                jnp.concatenate([query * (SCALE * g_cols[h]), key * scale_rest], axis=0), pairs[h]
            )
            conv_back(
                m, 0, h, later, queries[h][2],
                queries[h][1] * (d_query - query * jnp.sum(query * d_query, axis=-1, keepdims=True)),
            )
            conv_back(
                m, 1, h, later, keys[h][2],
                keys[h][1] * (d_key - key * jnp.sum(key * d_key, axis=-1, keepdims=True)),
            )
            conv_back(m, 2, h, later, values[h][2], b_cols[h] * d_rests[h] * values[h][1])
        d_log = mm_exact(upper, d_decay - d_decay_lines.T)
        d_arg = d_log * scal_ref[0:1, :] * sigmoid(small + scal_ref[1:2, :])
        dscal_ref[0:1, :] += jnp.sum(d_log * log_alpha, axis=0, keepdims=True)
        dscal_ref[1:2, :] += jnp.sum(d_arg, axis=0, keepdims=True)
        draw_ref[0, m, :, 4 * width : 4 * width + LANES] = (
            d_arg + d_beta * beta * (1.0 - beta)
        ).astype(BF)


def mixer_shapes(raw):
    blocks, group, rows, total = raw.shape
    heads = (total - LANES) // (4 * HD)
    return blocks, group, rows, heads, heads * HD, total


def whole(shape):
    return pl.BlockSpec(shape, lambda c, place: (0,) * len(shape))


PARAMS = dict(dimension_semantics=("arbitrary",), vmem_limit_bytes=56 * 1024 * 1024)


def mixer_forward(place, raw, aux, segrow, conv_rows, scal, gain):
    blocks, group, rows, heads, width, total = mixer_shapes(raw)
    at = lambda c, place: (place[c], 0, 0, 0)
    seq = lambda c, place: (c, 0, 0, 0)
    seq5 = lambda c, place: (c, 0, 0, 0, 0)
    fact = lambda c, place: (0, c, 0, 0)

    def body(*refs):
        forward_kernel(heads, *refs)

    return pl.pallas_call(
        body,
        grid_spec=pltpu.PrefetchScalarGridSpec(
            num_scalar_prefetch=1,
            grid=(blocks,),
            in_specs=[
                pl.BlockSpec((1, group, rows, total), at),
                pl.BlockSpec((group, 1, rows, 16), fact),
                pl.BlockSpec((group, 1, 8, rows), fact),
                whole(conv_rows.shape),
                whole(scal.shape),
                whole(gain.shape),
            ],
            out_specs=[
                pl.BlockSpec((1, group, rows, width), at),
                pl.BlockSpec((1, group, rows, width), seq),
                pl.BlockSpec((1, group, heads, rows, rows), seq5),
                pl.BlockSpec((1, group, rows, width), seq),
                pl.BlockSpec((1, group, heads, HD, HD), seq5),
            ],
            scratch_shapes=[
                pltpu.VMEM((group, rows + 8, 3 * width), F32),
                pltpu.VMEM((group, heads, HD, HD), F32),
            ],
        ),
        out_shape=[
            jax.ShapeDtypeStruct((blocks, group, rows, width), BF),
            jax.ShapeDtypeStruct((blocks, group, rows, width), F32),
            jax.ShapeDtypeStruct((blocks, group, heads, rows, rows), BF),
            jax.ShapeDtypeStruct((blocks, group, rows, width), BF),
            jax.ShapeDtypeStruct((blocks, group, heads, HD, HD), BF),
        ],
        compiler_params=pltpu.CompilerParams(**PARAMS),
        cost_estimate=pl.CostEstimate(
            flops=FORWARD_COST * blocks * group * heads, bytes_accessed=8_000_000, transcendentals=0
        ),
        name="mixer_forward",
    )(place, raw, aux, segrow, conv_rows, scal, gain)


def mixer_backward(place, raw, aux, segrow, conv_rows, scal, gain, d_mixed, saved):
    blocks, group, rows, heads, width, total = mixer_shapes(raw)
    core, inverse, update, states = saved
    back = lambda c: blocks - 1 - c
    at = lambda c, place: (place[back(c)], 0, 0, 0)
    before = lambda c, place: (place[jnp.maximum(back(c) - 1, 0)], 0, rows // 8 - 1, 0)
    seq = lambda c, place: (back(c), 0, 0, 0)
    seq5 = lambda c, place: (back(c), 0, 0, 0, 0)
    fact = lambda c, place: (0, back(c), 0, 0)

    def body(*refs):
        backward_kernel(heads, *refs)

    return pl.pallas_call(
        body,
        grid_spec=pltpu.PrefetchScalarGridSpec(
            num_scalar_prefetch=1,
            grid=(blocks,),
            in_specs=[
                pl.BlockSpec((1, group, rows, total), at),
                pl.BlockSpec((1, group, 8, total), before),
                pl.BlockSpec((group, 1, rows, 16), fact),
                pl.BlockSpec((group, 1, 8, rows), fact),
                whole(conv_rows.shape),
                whole(scal.shape),
                whole(gain.shape),
                pl.BlockSpec((1, group, rows, width), at),
                pl.BlockSpec((1, group, rows, width), seq),
                pl.BlockSpec((1, group, heads, rows, rows), seq5),
                pl.BlockSpec((1, group, rows, width), seq),
                pl.BlockSpec((1, group, heads, HD, HD), seq5),
            ],
            out_specs=[
                pl.BlockSpec((1, group, rows, total), at),
                whole((96, width)),
                whole((8, LANES)),
                whole((8, width)),
            ],
            scratch_shapes=[
                pltpu.VMEM((group, rows + 8, 3 * width), F32),
                pltpu.VMEM((group, rows + 8, 3 * width), F32),
                pltpu.VMEM((group, heads, HD, HD), F32),
            ],
        ),
        out_shape=[
            jax.ShapeDtypeStruct((blocks, group, rows, total), BF),
            jax.ShapeDtypeStruct((96, width), F32),
            jax.ShapeDtypeStruct((8, LANES), F32),
            jax.ShapeDtypeStruct((8, width), F32),
        ],
        compiler_params=pltpu.CompilerParams(**PARAMS),
        cost_estimate=pl.CostEstimate(
            flops=BACKWARD_COST * blocks * group * heads, bytes_accessed=12_000_000, transcendentals=0
        ),
        name="mixer_backward",
    )(place, raw, raw, aux, segrow, conv_rows, scal, gain, d_mixed, core, inverse, update, states)


def hop(values, bit, axis="head"):
    size = lax.axis_size(axis)
    return lax.ppermute(values, axis, [(i, i ^ bit) for i in range(size)])


def after(values, *earlier):
    kept = [item for group in earlier for item in (group if isinstance(group, list) else [group])]
    if not kept:
        return values
    return lax.optimization_barrier((values, *kept))[0]


def butterfly(values, axes):
    for axis in axes:
        bit = 1
        while bit < lax.axis_size(axis):
            values = values + hop(values, bit, axis)
            bit *= 2
    return values


def gather_near(values, *earlier):
    if earlier:
        values = after(values, *earlier)
    if lax.axis_size("head") != 4:
        return [lax.all_gather(values, "head", axis=0, tiled=True)]
    return [values, hop(values, 1), hop(values, 2)]


def gather_far(near, *earlier):
    if len(near) == 1:
        return []
    half = near[0].shape[0] // 2
    return [hop(after(near[2][:half], *earlier), 1), hop(after(near[1][half:], *earlier), 2)]


def block_parts(size, rows):
    if size != 4:
        return [[(0, r * rows, rows)] for r in range(size)]
    half = rows // 2
    return [[(0, 0, rows)], [(1, 0, rows)], [(2, 0, rows)], [(3, 0, half), (4, 0, half)]]


def joined(arrays):
    return arrays[0] if len(arrays) == 1 else jnp.concatenate(arrays, axis=0)


def scatter_plan(size, rows):
    half = rows // 2
    if size != 4:
        return [size * rows], {(r, h): (0, r * rows + h * half) for r in range(size) for h in (0, 1)}
    return [rows, rows, 2 * rows], {
        (1, 0): (0, 0), (3, 0): (0, half),
        (2, 1): (1, 0), (3, 1): (1, half),
        (0, 0): (2, 0), (0, 1): (2, half), (2, 0): (2, 2 * half), (1, 1): (2, 3 * half),
    }


def scatter_near(arrays, *earlier):
    if len(arrays) == 1:
        part = after(arrays[0], *earlier)
        return [lax.psum_scatter(part, "head", scatter_dimension=0, tiled=True)]
    to_x, to_y, keep = arrays
    return [hop(after(to_x, *earlier), 1), hop(after(to_y, *earlier), 2), keep]


def scatter_far(near, *earlier):
    if len(near) == 1:
        return near[0].astype(F32)
    in_x, in_y, keep = near
    half = in_x.shape[0] // 2
    keep = after(keep, *earlier)
    pass_y = (keep[2 * half : 3 * half].astype(F32) + in_x[half:].astype(F32)).astype(BF)
    pass_x = (keep[3 * half :].astype(F32) + in_y[half:].astype(F32)).astype(BF)
    last_y = hop(pass_y, 2).astype(F32)
    last_x = hop(pass_x, 1).astype(F32)
    near_sum = jnp.concatenate([in_x[:half], in_y[:half]], axis=0).astype(F32)
    last = jnp.concatenate([last_y, last_x], axis=0)
    return keep[: 2 * half].astype(F32) + near_sum + last


def scatter_kernel(size, where, transposed, x_ref, w_ref, *refs):
    outs, buf, sem = refs[:-2], refs[-2], refs[-1]
    step = pl.program_id(0)
    half = x_ref.shape[0] // 2
    slot = lax.rem(step, 2)

    def stores(block):
        return [
            pltpu.make_async_copy(
                buf.at[block % 2, h * half : (h + 1) * half],
                outs[where[(block, h)][0]].at[where[(block, h)][1] : where[(block, h)][1] + half],
                sem.at[block % 2, h],
            )
            for h in (0, 1)
        ]

    for block in range(2, size):
        @pl.when(step == block)
        def _(block=block):
            for copy in stores(block - 2):
                copy.wait()

    x = x_ref[...]
    buf[slot] = (mm_nt(x, w_ref[...]) if transposed else mm(x, w_ref[...])).astype(BF)
    for block in range(size):
        @pl.when(step == block)
        def _(block=block):
            for copy in stores(block):
                copy.start()
            if block == size - 1:
                for earlier in range(max(0, size - 2), size):
                    for copy in stores(earlier):
                        copy.wait()


def scatter_matmul(values, weight, size, transposed=False):
    rows = values.shape[0] // size
    width = weight.shape[0] if transposed else weight.shape[1]
    counts, where = scatter_plan(size, rows)
    return list(pl.pallas_call(
        lambda *refs: scatter_kernel(size, where, transposed, *refs),
        grid=(size,),
        in_specs=[
            pl.BlockSpec((rows, values.shape[1]), lambda i: (i, 0)),
            pl.BlockSpec(weight.shape, lambda i: (0, 0)),
        ],
        out_specs=[pl.BlockSpec(memory_space=pl.ANY)] * len(counts),
        out_shape=[jax.ShapeDtypeStruct((count, width), BF) for count in counts],
        scratch_shapes=[pltpu.VMEM((2, rows, width), BF), pltpu.SemaphoreType.DMA((2, 2))],
        compiler_params=pltpu.CompilerParams(**PARAMS),
        cost_estimate=pl.CostEstimate(
            flops=4 * values.size * width, bytes_accessed=15_000_000, transcendentals=0
        ),
        name="scatter_matmul",
    )(values, weight))


def ffn_kernel(turns, rows, parts, n_pieces, where, n_out, aliased, *refs):
    mids, cots = refs[:n_pieces], refs[n_pieces : 2 * n_pieces]
    wg_ref, wu_ref, wd_ref = refs[2 * n_pieces : 2 * n_pieces + 3]
    refs = refs[2 * n_pieces + 3 + (2 * n_out if aliased else 0) :]
    act_ref, dg_ref, du_ref, xo_ref, co_ref = refs[:5]
    gm_refs, ff_refs = refs[5 : 5 + n_out], refs[5 + n_out : 5 + 2 * n_out]
    wg, wu, wd, xbuf, cbuf, gm_buf, ff_buf, w_sem, x_sem, c_sem, o_sem = refs[5 + 2 * n_out :]
    step = pl.program_id(0)
    half = rows // 2
    steps = len(turns)

    def loads(turn):
        slot = turn % 2
        found = []
        for arrays, buf, sem in ((mids, xbuf, x_sem), (cots, cbuf, c_sem)):
            place = 0
            for k, (index, at, count) in enumerate(parts[turns[turn]]):
                found.append(
                    pltpu.make_async_copy(
                        arrays[index].at[at : at + count],
                        buf.at[slot, place : place + count],
                        sem.at[slot, k],
                    )
                )
                place += count
        return found

    def stores(turn):
        slot = turn % 2
        found = []
        for k, (buf, outs) in enumerate(((gm_buf, gm_refs), (ff_buf, ff_refs))):
            for h in (0, 1):
                index, at = where[(turns[turn], h)]
                found.append(
                    pltpu.make_async_copy(
                        buf.at[slot, h * half : (h + 1) * half],
                        outs[index].at[at : at + half],
                        o_sem.at[slot, 2 * k + h],
                    )
                )
        return found

    weights = [
        pltpu.make_async_copy(src, dst, w_sem.at[k])
        for k, (src, dst) in enumerate(((wg_ref, wg), (wu_ref, wu), (wd_ref, wd)))
    ]

    @pl.when(step == 0)
    def _():
        for copy in loads(0):
            copy.start()
        for copy in weights:
            copy.start()

    for turn in range(steps):
        @pl.when(step == turn)
        def _(turn=turn):
            if turn + 1 < steps:
                for copy in loads(turn + 1):
                    copy.start()
            for copy in loads(turn):
                copy.wait()
            if turn >= 2:
                for copy in stores(turn - 2):
                    copy.wait()

    slot = lax.rem(step, 2)

    @pl.when(step == 0)
    def _():
        weights[0].wait()

    x = xbuf[slot]
    gate = jnp.dot(x, wg[...], preferred_element_type=F32)

    @pl.when(step == 0)
    def _():
        weights[1].wait()

    upward = jnp.dot(x, wu[...], preferred_element_type=F32)

    @pl.when(step == 0)
    def _():
        weights[2].wait()

    cot = cbuf[slot]
    d_act = jnp.dot(cot, wd[...], preferred_element_type=F32)
    open_ = sigmoid(gate)
    silu = gate * open_
    act = (silu * upward).astype(BF)
    d_gate = (d_act * upward * open_ * (1.0 + gate * (1.0 - open_))).astype(BF)
    d_up = (d_act * silu).astype(BF)
    act_ref[0] = act
    dg_ref[0] = d_gate
    du_ref[0] = d_up
    xo_ref[0] = x
    co_ref[0] = cot
    gm_buf[slot] = (mm_nt(d_gate, wg[...]) + mm_nt(d_up, wu[...])).astype(BF)
    ff_buf[slot] = mm_nt(act, wd[...]).astype(BF)
    for turn in range(steps):
        @pl.when(step == turn)
        def _(turn=turn):
            for copy in stores(turn):
                copy.start()
            if turn == steps - 1:
                for earlier in range(max(0, steps - 2), steps):
                    for copy in stores(earlier):
                        copy.wait()


def ffn_stage(turns, mids, cots, weights, size, filled=None):
    width, hidden = weights[0].shape
    rows = mids[0].shape[0] if size == 4 else mids[0].shape[0] // size
    parts = block_parts(size, rows)
    counts, where = scatter_plan(size, rows)
    aliased = filled is not None
    filled = list(filled) if aliased else []

    def body(*refs):
        ffn_kernel(turns, rows, parts, len(mids), where, len(counts), aliased, *refs)

    anywhere = pl.BlockSpec(memory_space=pl.ANY)
    by_block = lambda last: pl.BlockSpec((1, rows, last), lambda i: (i, 0, 0))
    steps = len(turns)
    first = 2 * len(mids) + 3
    out = pl.pallas_call(
        body,
        grid=(steps,),
        in_specs=[anywhere] * (first + len(filled)),
        out_specs=[by_block(hidden)] * 3 + [by_block(width)] * 2 + [anywhere] * (2 * len(counts)),
        out_shape=[jax.ShapeDtypeStruct((steps, rows, hidden), BF)] * 3
        + [jax.ShapeDtypeStruct((steps, rows, width), BF)] * 2
        + [jax.ShapeDtypeStruct((c, width), BF) for c in counts] * 2,
        input_output_aliases={first + k: 5 + k for k in range(len(filled))},
        scratch_shapes=[
            pltpu.VMEM((width, hidden), BF),
            pltpu.VMEM((width, hidden), BF),
            pltpu.VMEM((width, hidden), BF),
            pltpu.VMEM((2, rows, width), BF),
            pltpu.VMEM((2, rows, width), BF),
            pltpu.VMEM((2, rows, width), BF),
            pltpu.VMEM((2, rows, width), BF),
            pltpu.SemaphoreType.DMA((3,)),
            pltpu.SemaphoreType.DMA((2, 2)),
            pltpu.SemaphoreType.DMA((2, 2)),
            pltpu.SemaphoreType.DMA((2, 4)),
        ],
        compiler_params=pltpu.CompilerParams(**PARAMS),
        cost_estimate=pl.CostEstimate(
            flops=steps * rows * width * hidden * 20, bytes_accessed=30_000_000, transcendentals=0
        ),
        name="ffn_stage",
    )(*mids, *cots, *weights, *filled)
    flat = [array.reshape(steps * rows, array.shape[-1]) for array in out[:5]]
    return flat, list(out[5:])


def piece_kernel(size, parts, n_pieces, transposed, *refs):
    pieces, w_ref, out_ref, copy_ref, xbuf, x_sem = refs[:n_pieces], *refs[n_pieces:]
    step = pl.program_id(0)

    def loads(block):
        slot = block % 2
        found, place = [], 0
        for k, (index, at, count) in enumerate(parts[block]):
            found.append(
                pltpu.make_async_copy(
                    pieces[index].at[at : at + count],
                    xbuf.at[slot, place : place + count],
                    x_sem.at[slot, k],
                )
            )
            place += count
        return found

    for block in range(size):
        @pl.when(step == block)
        def _(block=block):
            if block == 0:
                for copy in loads(0):
                    copy.start()
            if block + 1 < size:
                for copy in loads(block + 1):
                    copy.start()
            for copy in loads(block):
                copy.wait()

    x = xbuf[lax.rem(step, 2)]
    copy_ref[0] = x
    out_ref[0] = mm_nt(x, w_ref[...]) if transposed else mm(x, w_ref[...])


def piece_matmul(pieces, weight, size, transposed=False):
    width = pieces[0].shape[1]
    rows = pieces[0].shape[0] if size == 4 else pieces[0].shape[0] // size
    columns = weight.shape[0] if transposed else weight.shape[1]
    parts = block_parts(size, rows)
    return pl.pallas_call(
        lambda *refs: piece_kernel(size, parts, len(pieces), transposed, *refs),
        grid=(size,),
        in_specs=[pl.BlockSpec(memory_space=pl.ANY)] * len(pieces)
        + [pl.BlockSpec(weight.shape, lambda i: (0, 0))],
        out_specs=[
            pl.BlockSpec((1, rows, columns), lambda i: (i, 0, 0)),
            pl.BlockSpec((1, rows, width), lambda i: (i, 0, 0)),
        ],
        out_shape=[
            jax.ShapeDtypeStruct((size, rows, columns), F32),
            jax.ShapeDtypeStruct((size, rows, width), BF),
        ],
        scratch_shapes=[pltpu.VMEM((2, rows, width), BF), pltpu.SemaphoreType.DMA((2, 2))],
        compiler_params=pltpu.CompilerParams(**PARAMS),
        cost_estimate=pl.CostEstimate(
            flops=4 * size * rows * width * columns, bytes_accessed=30_000_000, transcendentals=0
        ),
        name="piece_matmul",
    )(*pieces, weight)


def wgrad_kernel(count, *refs):
    lefts, rights, rest = refs[:count], refs[count : 2 * count], refs[2 * count :]
    total = mm_tn(lefts[0][...], rights[0][...])
    for left, right in zip(lefts[1:], rights[1:]):
        total = total + mm_tn(left[...], right[...])
    out_ref = rest[-1]
    if len(rest) == 1:
        out_ref[...] = total.astype(BF)
    else:
        columns = total.shape[1]
        out_ref[:, :columns] = total.astype(BF)
        out_ref[:, columns:] = rest[0][...]


def weight_gradient(lefts, rights, beside=None):
    wide = lefts[0].shape[1]
    columns = rights[0].shape[1]
    extra = [] if beside is None else [beside]
    full = columns + sum(item.shape[1] for item in extra)
    tile = 512 if wide % 512 == 0 else wide
    count = len(lefts)
    depth = sum(left.shape[0] for left in lefts)
    return pl.pallas_call(
        lambda *refs: wgrad_kernel(count, *refs),
        grid=(wide // tile,),
        in_specs=[pl.BlockSpec((left.shape[0], tile), lambda i: (0, i)) for left in lefts]
        + [pl.BlockSpec(right.shape, lambda i: (0, 0)) for right in rights]
        + [pl.BlockSpec((tile, item.shape[1]), lambda i: (i, 0)) for item in extra],
        out_specs=pl.BlockSpec((tile, full), lambda i: (i, 0)),
        out_shape=jax.ShapeDtypeStruct((wide, full), BF),
        compiler_params=pltpu.CompilerParams(**PARAMS),
        cost_estimate=pl.CostEstimate(
            flops=3 * depth * wide * columns, bytes_accessed=20_000_000, transcendentals=0
        ),
        name="weight_gradient",
    )(*lefts, *rights, *extra)


def block_places(size):
    base = lax.iota(jnp.int32, size)
    if size != 4:
        return base
    return base ^ lax.axis_index("head").astype(jnp.int32)


def contract_rows(left, right):
    return lax.dot_general(left, right, (((0,), (0,)), ((), ())), preferred_element_type=F32)


def contract_cols(left, right):
    return lax.dot_general(left, right, (((1,), (1,)), ((), ())), preferred_element_type=F32)


def times(left, right):
    return jnp.dot(left, right, preferred_element_type=F32)


def sequence_facts(doc_lengths, blocks, rows):
    span = blocks * rows
    ends = jnp.cumsum(doc_lengths, axis=-1)
    places = lax.iota(jnp.int32, span)
    segment = jnp.sum((places[None, :, None] >= ends[:, None, :]).astype(jnp.int32), axis=-1)
    columns = [segment]
    for j in range(1, 4):
        columns.append(
            (jnp.pad(segment, ((0, 0), (j, 0)), constant_values=-1)[:, :-j] == segment)
        )
    by_chunk = segment.reshape(-1, blocks, rows)
    prior = jnp.pad(by_chunk[:, :-1, -1], ((0, 0), (1, 0)), constant_values=-1)
    columns.append((by_chunk == prior[:, :, None]).reshape(segment.shape))
    columns.append((by_chunk == by_chunk[:, :, -1:]).reshape(segment.shape))
    columns += [jnp.zeros_like(segment)] * 2
    for j in range(1, 4):
        columns.append(
            (jnp.pad(segment, ((0, 0), (0, j)), constant_values=-1)[:, j:] == segment)
        )
    columns += [jnp.zeros_like(segment)] * (16 - len(columns))
    aux = jnp.stack([item.astype(F32) for item in columns], axis=-1)
    aux = aux.reshape(-1, blocks, rows, 16)
    lines = jnp.broadcast_to(by_chunk.astype(F32)[:, :, None, :], by_chunk.shape[:2] + (8, rows))
    return aux, lines


def on_device(
    tokens, cotangent, token_counts, doc_lengths, norm_in, w_query, w_key, w_value, w_outgate,
    w_decay, w_beta, conv_weight, decay_log, dt_bias, gain_out, w_out, norm_mid, w_gate, w_up,
    w_down,
):
    micro_count, rows, width = tokens.shape
    blocks = lax.axis_size("head")
    group = micro_count // 2
    own_rows = group * rows
    span = own_rows * blocks
    heads = decay_log.shape[0]
    own = heads * HD
    groups = range(micro_count // group)
    my_places = lax.axis_index("head") * rows + lax.iota(jnp.int32, rows)
    live = (my_places[None, :] < token_counts[:, :1]).astype(F32)[:, :, None]
    place = block_places(blocks)
    aux, lines = sequence_facts(doc_lengths[:, 0], blocks, rows)
    conv_rows = jnp.pad(conv_weight.reshape(12, own), ((0, 4), (0, 0)))
    scal = jnp.zeros((8, LANES), F32)
    scal = scal.at[0, :heads].set(-jnp.exp(decay_log)).at[1, :heads].set(dt_bias)
    gain_row = jnp.broadcast_to(gain_out[None], (8, own))
    ffn_gate = lax.all_gather(w_gate, "dp", axis=0, tiled=True)
    ffn_up = lax.all_gather(w_up, "dp", axis=0, tiled=True)
    ffn_down = lax.all_gather(w_down, "dp", axis=0, tiled=True)

    def of_group(array, i):
        return array[i * group : (i + 1) * group]

    inputs, grads, lives, pulls_in, normed_in = [], [], [], [], []
    for i in groups:
        x = of_group(tokens, i).reshape(own_rows, width).astype(F32)
        normed, pull = jax.vjp(norm_rows, x, norm_in)
        inputs.append(x)
        pulls_in.append(pull)
        normed_in.append(normed.astype(BF))
        grads.append((of_group(cotangent, i).astype(F32) * of_group(live, i)).reshape(own_rows, width))
    cots = [item.astype(BF) for item in grads]
    in_a1 = gather_near(normed_in[0])
    w_in = jnp.concatenate(
        [w_query, w_key, w_value, w_outgate, w_decay, w_beta,
         jnp.zeros((width, LANES - 2 * heads), BF)], axis=1
    )

    def project(pieces):
        raw, full = piece_matmul(pieces, w_in, blocks)
        return raw.reshape(blocks, group, rows, 4 * own + LANES), full.reshape(span, width)

    def mix(raw, i):
        mixed, *saved = mixer_forward(
            place, raw, of_group(aux, i), of_group(lines, i), conv_rows, scal, gain_row
        )
        return mixed.reshape(span, own), saved

    def out_of(mixed):
        return scatter_matmul(mixed, w_out, blocks)

    def middle(i, attn):
        resid = inputs[i] + attn
        normed, pull = jax.vjp(norm_rows, resid, norm_mid)
        return resid, pull, normed.astype(BF)

    in_a2 = gather_far(in_a1)
    in_b1 = gather_near(normed_in[1], in_a2)
    raw_a, full_a = project(in_a1 + in_a2)
    in_b2 = gather_far(in_b1, raw_a)
    cot_a1 = gather_near(cots[0], in_b1)
    mixed_a, saved_a = mix(after(raw_a, in_b1), 0)
    attn_a = out_of(after(mixed_a, in_b2))
    at_a1 = scatter_near(attn_a)
    pieces_b = in_b1 + in_b2
    raw_b, full_b = project([after(pieces_b[0], attn_a, cot_a1)] + pieces_b[1:])
    sum_a = scatter_far(at_a1, raw_b)
    cot_a2 = gather_far(cot_a1, raw_b)
    mixed_b, saved_b = mix(after(raw_b, at_a1), 1)
    resid_a, pull_a, mid_a = middle(0, sum_a)
    mid_a1 = gather_near(mid_a)
    attn_b = out_of(after(mixed_b, mid_a, cot_a2))
    at_b1 = scatter_near(attn_b, mid_a1)
    mid_a2 = gather_far(mid_a1, attn_b)

    ffn_weights = [ffn_gate, ffn_up, ffn_down]
    first_turns = (1, 3) if blocks == 4 else tuple(range(blocks // 2))
    last_turns = tuple(r for r in range(blocks) if r not in first_turns)
    outs = len(scatter_plan(blocks, own_rows)[0])
    near_a = mid_a1 + mid_a2
    near_a[0] = after(near_a[0], at_b1)
    sum_b = scatter_far(at_b1)
    cot_b1 = gather_near(cots[1], at_b1)
    kept_a, begun = ffn_stage(first_turns, near_a, cot_a1 + cot_a2, ffn_weights, blocks)
    resid_b, pull_b, mid_b = middle(1, sum_b)
    mid_b1 = gather_near(mid_b, kept_a[0])
    cot_b2 = gather_far(cot_b1, kept_a[0])
    begun[0] = after(begun[0], mid_b, cot_b1)
    kept_a2, out_a = ffn_stage(
        last_turns, near_a, cot_a1 + cot_a2, ffn_weights, blocks, begun
    )
    mid_b2 = gather_far(mid_b1, kept_a2[0], cot_b2)
    gm_a1 = scatter_near(out_a[:outs], mid_b2)
    near_b = mid_b1 + mid_b2
    near_b[0] = after(near_b[0], out_a[0])
    kept_b, begun = ffn_stage(first_turns, near_b, cot_b1 + cot_b2, ffn_weights, blocks)
    d_mid_a = scatter_far(gm_a1, kept_b[0])
    begun = [after(begun[0], gm_a1)] + begun[1:]
    kept_b2, out_b = ffn_stage(last_turns, near_b, cot_b1 + cot_b2, ffn_weights, blocks, begun)
    kept = [kept_a, kept_a2, kept_b, kept_b2]
    acts, gates, ups, mids, cot_all = [[item[k] for item in kept] for k in range(5)]

    def share(term):
        return lax.psum_scatter(term, "dp", scatter_dimension=0, tiled=True).astype(F32)

    def resid_back(i, pull, d_mid):
        d_resid, d_norm = pull(d_mid)
        d_resid = grads[i] + d_resid
        return d_resid, d_norm, d_resid.astype(BF)

    gm_b1 = scatter_near(out_b[:outs], d_mid_a)
    d_resid_a, gain_mid_a, low_a = resid_back(0, pull_a, d_mid_a)
    rg_a1 = gather_near(low_a)
    gates[0] = after(gates[0], low_a)
    term_gate = weight_gradient(mids, gates)
    grad_gate = share(term_gate)
    rg_a2 = gather_far(rg_a1, term_gate)
    d_mid_b = scatter_far(gm_b1, term_gate)
    ups[0] = after(ups[0], term_gate, rg_a1, gm_b1)
    term_up = weight_gradient(mids, ups)
    grad_up = share(term_up)
    d_resid_b, gain_mid_b, low_b = resid_back(1, pull_b, after(d_mid_b, term_up))
    rg_b1 = gather_near(low_b)
    ff_a1 = scatter_near(out_a[outs:], low_b)

    def to_mixed(pieces):
        d_mixed, full = piece_matmul(pieces, w_out, blocks, transposed=True)
        return d_mixed.reshape(blocks, group, rows, own), full.reshape(span, width)

    def mix_back(i, d_mixed, raw, saved):
        d_raw, *sums = mixer_backward(
            place, raw, of_group(aux, i), of_group(lines, i), conv_rows, scal, gain_row,
            d_mixed, saved,
        )
        return d_raw.reshape(span, 4 * own + LANES), sums

    def in_back(d_raw):
        return scatter_matmul(d_raw, w_in, blocks, transposed=True)

    pieces_ra = rg_a1 + rg_a2
    pieces_ra[0] = after(pieces_ra[0], low_b)
    d_mixed_a, full_ra = to_mixed(pieces_ra)
    d_raw_a, sums_a = mix_back(0, d_mixed_a, raw_a, saved_a)
    rg_b2 = gather_far(rg_b1, d_raw_a)
    ffn_a = scatter_far(ff_a1, d_raw_a)
    d_in_a = in_back(after(d_raw_a, ff_a1, rg_b1))
    gi_a1 = scatter_near(d_in_a)
    pieces_rb = rg_b1 + rg_b2
    pieces_rb[0] = after(pieces_rb[0], d_in_a, ffn_a)
    d_mixed_b, full_rb = to_mixed(pieces_rb)
    acts[0] = after(acts[0], d_mixed_b)
    term_down = weight_gradient(cot_all, acts)
    term_out = weight_gradient(
        [full_ra, full_rb], [after(mixed_a, gi_a1), mixed_b], term_down
    )
    shared_out = share(term_out)
    grad_out, grad_down = shared_out[:, :own].T, shared_out[:, own:]
    ff_b1 = scatter_near(out_b[outs:], term_out)
    d_raw_b, sums_b = mix_back(1, after(d_mixed_b, term_out), raw_b, saved_b)
    term_in = weight_gradient([full_a, full_b], [d_raw_a, after(d_raw_b, ff_b1)])
    grad_in = share(term_in)
    d_norm_a = scatter_far(gi_a1, term_in)
    ffn_b = scatter_far(ff_b1, term_in)
    d_in_b = in_back(after(d_raw_b, term_in))
    gi_b1 = scatter_near(d_in_b, d_norm_a, ffn_b)
    d_norm_b = scatter_far(gi_b1)

    results, input_grads = [], []
    gain_in = jnp.zeros_like(norm_in)
    for i, (resid, ffn, d_resid, d_norm) in enumerate(
        ((resid_a, ffn_a, d_resid_a, d_norm_a), (resid_b, ffn_b, d_resid_b, d_norm_b))
    ):
        results.append((resid + ffn).astype(BF).reshape(group, rows, width))
        d_inputs, d_gain = pulls_in[i](d_norm)
        input_grads.append((d_inputs + d_resid).astype(BF).reshape(group, rows, width))
        gain_in = gain_in + d_gain
    gain_mid = gain_mid_a + gain_mid_b
    small_sums = [left + right for left, right in zip(sums_a, sums_b)]
    conv_sum = jnp.sum(small_sums[0].reshape(12, 8, own), axis=1)
    scal_sum = jnp.pad(small_sums[1][:2, :heads], ((0, 0), (0, own - heads)))
    wide = jnp.concatenate([conv_sum, small_sums[2][:1], scal_sum, jnp.zeros((1, own), F32)], axis=0)
    wide = butterfly(after(wide, term_in), ("dp",))
    narrow = wide[13:15]
    gains = butterfly(jnp.stack([gain_in, gain_mid]), ("dp", "head"))
    return (
        jnp.concatenate(results, axis=0),
        jnp.concatenate(input_grads, axis=0),
        gains[0],
        grad_in[:, :own],
        grad_in[:, own : 2 * own],
        grad_in[:, 2 * own : 3 * own],
        grad_in[:, 3 * own : 4 * own],
        grad_in[:, 4 * own : 4 * own + heads],
        grad_in[:, 4 * own + heads : 4 * own + 2 * heads],
        wide[:12].reshape(conv_weight.shape),
        narrow[0, :heads],
        narrow[1, :heads],
        wide[12],
        grad_out,
        gains[1],
        grad_gate,
        grad_up,
        grad_down,
    )


def solution(mesh):
    return jax.shard_map(
        on_device,
        mesh=mesh,
        in_specs=(
            P(None, ("dp", "head"), None),
            P(None, ("dp", "head"), None),
            P(None, "dp"),
            P(None, "dp", None),
            P(),
            P(None, "head"),
            P(None, "head"),
            P(None, "head"),
            P(None, "head"),
            P(None, "head"),
            P(None, "head"),
            P(None, None, "head"),
            P("head"),
            P("head"),
            P("head"),
            P("head", None),
            P(),
            P("dp", "head"),
            P("dp", "head"),
            P("dp", "head"),
        ),
        out_specs=(
            P(None, ("dp", "head"), None),
            P(None, ("dp", "head"), None),
            P(),
            P("dp", "head"),
            P("dp", "head"),
            P("dp", "head"),
            P("dp", "head"),
            P("dp", "head"),
            P("dp", "head"),
            P(None, None, "head"),
            P("head"),
            P("head"),
            P("head"),
            P("head", "dp"),
            P(),
            P("dp", "head"),
            P("dp", "head"),
            P("dp", "head"),
        ),
        check_vma=False,
    )
```

```python
import jax
import jax.numpy as jnp
from jax import lax
from jax.experimental import pallas as pl
from jax.experimental.pallas import tpu as pltpu
from jax.sharding import PartitionSpec as P

HD = 128
LANES = 128
SCALE = HD ** (-0.5)
BF = jnp.bfloat16
F32 = jnp.float32
FORWARD_COST = 735_000_000
BACKWARD_COST = 1_650_000_000


def norm_rows(values, gain):
    return values * lax.rsqrt(jnp.mean(values * values, axis=-1, keepdims=True) + 1e-05) * gain


def swiglu(gate, upward):
    return jax.nn.silu(gate) * upward


def mm(left, right):
    return jnp.dot(left.astype(BF), right.astype(BF), preferred_element_type=F32)


def mm_nt(left, right):
    return lax.dot_general(
        left.astype(BF), right.astype(BF), (((1,), (1,)), ((), ())), preferred_element_type=F32
    )


def mm_tn(left, right):
    return lax.dot_general(
        left.astype(BF), right.astype(BF), (((0,), (0,)), ((), ())), preferred_element_type=F32
    )


def mm_exact(left, right):
    return jnp.dot(left, right, preferred_element_type=F32, precision=lax.Precision.HIGHEST)


def sigmoid(values):
    return 1.0 / (1.0 + jnp.exp(-values))


def softplus(values):
    return jnp.maximum(values, 0.0) + jnp.log1p(jnp.exp(-jnp.abs(values)))


def chunk_masks(rows):
    row_ids = lax.broadcasted_iota(jnp.int32, (rows, rows), 0)
    col_ids = lax.broadcasted_iota(jnp.int32, (rows, rows), 1)
    return row_ids, col_ids


def chunk_gates(small, scal_ref, aux, tri):
    rows = small.shape[0]
    log_alpha = scal_ref[0:1, :] * softplus(small + scal_ref[1:2, :])
    beta = sigmoid(small)
    decay_sum = mm_exact(tri, log_alpha)
    last = decay_sum[rows - 1 : rows, :]
    carried = aux[:, 4:5]
    growth = jnp.exp(decay_sum) * carried
    tail = jnp.exp(last - decay_sum) * aux[:, 5:6]
    keep = jnp.exp(last) * carried[rows - 1 : rows, :]
    return log_alpha, beta, decay_sum, growth, tail, keep


def spread_out(columns, index):
    return jnp.broadcast_to(columns[:, index : index + 1], (columns.shape[0], HD))


def conv_of(ext_ref, conv_ref, masks, m, index, head, rows, width):
    lanes = slice(index * width + head * HD, index * width + (head + 1) * HD)
    own = slice(head * HD, (head + 1) * HD)
    taps = [ext_ref[m, 8 : 8 + rows, lanes]]
    for j in range(1, 4):
        taps.append(ext_ref[m, 8 - j : 8 - j + rows, lanes] * masks[j - 1])
    total = taps[0] * conv_ref[4 * index : 4 * index + 1, own]
    for j in range(1, 4):
        total = total + taps[j] * conv_ref[4 * index + j : 4 * index + j + 1, own]
    return total, taps


def invert_unit_lower(powers, row_ids, col_ids):
    rows = row_ids.shape[0]
    eye = (row_ids == col_ids).astype(F32)
    pair = (row_ids // 2) == (col_ids // 2)
    inverses = [eye - jnp.where(pair, power, 0.0) for power in powers]
    half = 2
    while half < rows:
        joint = ((row_ids // (2 * half)) == (col_ids // (2 * half))) & (
            (row_ids // half) != (col_ids // half)
        )
        lows = [inverse.astype(BF) for inverse in inverses]
        firsts = [mm(low, jnp.where(joint, power, 0.0)) for low, power in zip(lows, powers)]
        inverses = [
            inverse - mm(first, low) for inverse, first, low in zip(inverses, firsts, lows)
        ]
        half *= 2
    return [inverse.astype(BF) for inverse in inverses]


def forward_kernel(
    heads, place_ref, raw_ref, aux_ref, segrow_ref, conv_ref, scal_ref, gain_ref,
    mixed_ref, core_ref, inv_ref, upd_ref, st_ref, ext_ref, state_ref,
):
    step = pl.program_id(0)
    group, rows = raw_ref.shape[1:3]
    width = heads * HD
    row_ids, col_ids = chunk_masks(rows)
    tri = (row_ids >= col_ids).astype(F32)
    strict = row_ids > col_ids

    @pl.when(step == 0)
    def _():
        ext_ref[:, 0:8, :] = jnp.zeros((group, 8, 3 * width), F32)
        state_ref[...] = jnp.zeros_like(state_ref)

    ext_ref[:, 8 : 8 + rows, :] = raw_ref[0, :, :, 0 : 3 * width]
    chains = [(m, h) for m in range(group) for h in range(heads)]
    stacked, values, powers, outs, betas, growths, tails, keeps = [], [], [], [], [], [], [], []
    for m in range(group):
        aux = aux_ref[m, 0]
        small = raw_ref[0, m, :, 4 * width : 4 * width + LANES]
        _, beta, decay_sum, growth, tail, keep = chunk_gates(small, scal_ref, aux, tri)
        masks = [spread_out(aux, j) for j in range(1, 4)]
        decay_rows = decay_sum.T
        below = (row_ids >= col_ids) & (aux[:, 0:1] == segrow_ref[m, 0, 0:1, :])
        for head in range(heads):
            query, _ = conv_of(ext_ref, conv_ref, masks, m, 0, head, rows, width)
            query = query * sigmoid(query)
            query = query * (
                lax.rsqrt(jnp.sum(query * query, axis=-1, keepdims=True) + 1e-06) * SCALE
            )
            key, _ = conv_of(ext_ref, conv_ref, masks, m, 1, head, rows, width)
            key = key * sigmoid(key)
            key = key * lax.rsqrt(jnp.sum(key * key, axis=-1, keepdims=True) + 1e-06)
            value, _ = conv_of(ext_ref, conv_ref, masks, m, 2, head, rows, width)
            value = value * sigmoid(value)
            b_col = spread_out(beta, heads + head)
            spread = decay_sum[:, head : head + 1] - decay_rows[head : head + 1, :]
            inside = jnp.exp(jnp.where(below, spread, -1e30))
            both = jnp.concatenate([key, query], axis=0).astype(BF)
            dots = mm_nt(both, both[:rows])
            stacked.append(both)
            values.append(value)
            powers.append(jnp.where(strict, b_col[:, :rows] * dots[:rows] * inside, 0.0))
            outs.append((dots[rows:] * inside).astype(BF))
            betas.append(b_col)
            growths.append(spread_out(growth, head))
            tails.append(spread_out(tail, head))
            keeps.append(keep[:, head : head + 1])
    inverses = invert_unit_lower(powers, row_ids, col_ids)
    states = [state_ref[m, h] for m, h in chains]
    lows = [state.astype(BF) for state in states]
    applied = [mm(both, low) for both, low in zip(stacked, lows)]
    updates = []
    for i, (m, h) in enumerate(chains):
        st_ref[0, m, h] = lows[i]
        inv_ref[0, m, h] = inverses[i]
        rest = betas[i] * (values[i] - growths[i] * applied[i][:rows])
        updates.append(mm(inverses[i], rest).astype(BF))
    for i, (m, h) in enumerate(chains):
        lanes = slice(h * HD, (h + 1) * HD)
        upd_ref[0, m, :, lanes] = updates[i]
        state_ref[m, h] = keeps[i] * states[i] + mm_tn(
            stacked[i][:rows].astype(F32) * tails[i], updates[i]
        )
        core = growths[i] * applied[i][rows:] + mm(outs[i], updates[i])
        core_ref[0, m, :, lanes] = core
        outgate = raw_ref[0, m, :, 3 * width + h * HD : 3 * width + (h + 1) * HD]
        normed = core * lax.rsqrt(jnp.mean(core * core, axis=-1, keepdims=True) + 1e-05)
        mixed_ref[0, m, :, lanes] = (
            normed * gain_ref[0:1, lanes] * (outgate * sigmoid(outgate))
        ).astype(BF)
    ext_ref[:, 0:8, :] = ext_ref[:, rows : rows + 8, :]


def backward_kernel(
    heads, place_ref, raw_ref, prev_ref, aux_ref, segrow_ref, conv_ref, scal_ref, gain_ref,
    dmix_ref, core_ref, inv_ref, upd_ref, st_ref,
    draw_ref, dconv_ref, dscal_ref, dgain_ref, ext_ref, dext_ref, dstate_ref,
):
    step = pl.program_id(0)
    group, rows = raw_ref.shape[1:3]
    width = heads * HD

    @pl.when(step == 0)
    def _():
        dext_ref[:, rows : rows + 8, :] = jnp.zeros((group, 8, 3 * width), F32)
        dstate_ref[...] = jnp.zeros_like(dstate_ref)
        dconv_ref[...] = jnp.zeros_like(dconv_ref)
        dscal_ref[...] = jnp.zeros_like(dscal_ref)
        dgain_ref[...] = jnp.zeros_like(dgain_ref)

    @pl.when(step > 0)
    def _():
        dext_ref[:, rows : rows + 8, :] = dext_ref[:, 0:8, :]

    ext_ref[:, 0:8, :] = prev_ref[0, :, :, 0 : 3 * width]
    ext_ref[:, 8 : 8 + rows, :] = raw_ref[0, :, :, 0 : 3 * width]
    row_ids, col_ids = chunk_masks(rows)
    tri = (row_ids >= col_ids).astype(F32)
    upper = (row_ids <= col_ids).astype(F32)
    strict = row_ids > col_ids
    lane_ids = lax.broadcasted_iota(jnp.int32, (rows, LANES), 1)
    line_ids = lax.broadcasted_iota(jnp.int32, (LANES, rows), 0)
    last_row = lax.broadcasted_iota(jnp.int32, (rows, 1), 0) == rows - 1

    def conv_back(m, index, head, later, taps, d_conv):
        lanes = slice(index * width + head * HD, index * width + (head + 1) * HD)
        own = slice(head * HD, (head + 1) * HD)
        dext_ref[m, 0:rows, lanes] = d_conv
        total = d_conv * conv_ref[4 * index : 4 * index + 1, own]
        for j in range(4):
            line = 4 * index + j
            dconv_ref[8 * line : 8 * line + 8, own] += jnp.sum(
                (d_conv * taps[j]).reshape(rows // 8, 8, HD), axis=0
            )
        for j in range(1, 4):
            line = slice(4 * index + j, 4 * index + j + 1)
            total = total + dext_ref[m, j : j + rows, lanes] * conv_ref[line, own] * later[j - 1]
        draw_ref[0, m, :, lanes] = total.astype(BF)

    for m in range(group):
        aux = aux_ref[m, 0]
        small = raw_ref[0, m, :, 4 * width : 4 * width + LANES]
        log_alpha, beta, decay_sum, growth, tail, keep = chunk_gates(small, scal_ref, aux, tri)
        masks = [spread_out(aux, j) for j in range(1, 4)]
        later = [spread_out(aux, 7 + j) for j in range(1, 4)]
        decay_rows = decay_sum.T
        below = (row_ids >= col_ids) & (aux[:, 0:1] == segrow_ref[m, 0, 0:1, :])
        d_decay = jnp.zeros((rows, LANES), F32)
        d_beta = jnp.zeros((rows, LANES), F32)
        d_decay_lines = jnp.zeros((LANES, rows), F32)
        everyone = range(heads)
        own_lanes = [slice(h * HD, (h + 1) * HD) for h in everyone]
        b_cols = [spread_out(beta, heads + h) for h in everyone]
        g_cols = [spread_out(growth, h) for h in everyone]
        t_cols = [spread_out(tail, h) for h in everyone]
        keeps = [keep[:, h : h + 1] for h in everyone]
        d_cores, queries, keys, values = [], [], [], []
        for h in everyone:
            lanes = own_lanes[h]
            gate_lanes = slice(3 * width + h * HD, 3 * width + (h + 1) * HD)
            outgate = raw_ref[0, m, :, gate_lanes]
            gate = sigmoid(outgate)
            core = core_ref[0, m, :, lanes]
            inv_norm = lax.rsqrt(jnp.mean(core * core, axis=-1, keepdims=True) + 1e-05)
            normed = core * inv_norm
            d_mixed = dmix_ref[0, m, :, lanes].astype(F32)
            gain = gain_ref[0:1, lanes]
            d_silu = d_mixed * (outgate * gate)
            dgain_ref[0:1, lanes] += jnp.sum(d_silu * normed, axis=0, keepdims=True)
            draw_ref[0, m, :, gate_lanes] = (
                d_mixed * normed * gain * (gate * (1.0 + outgate * (1.0 - gate)))
            ).astype(BF)
            d_normed = d_silu * gain
            d_cores.append(
                (inv_norm * (d_normed - normed * jnp.mean(d_normed * normed, axis=-1, keepdims=True))).astype(BF)
            )
            parts = []
            for index in range(3):
                conv, taps = conv_of(ext_ref, conv_ref, masks, m, index, h, rows, width)
                gate = sigmoid(conv)
                act = conv * gate
                slope = gate * (1.0 + conv * (1.0 - gate))
                if index == 2:
                    parts.append((act, slope, taps))
                else:
                    root = lax.rsqrt(jnp.sum(act * act, axis=-1, keepdims=True) + 1e-06)
                    parts.append((act * root, slope * root, taps))
            queries.append(parts[0])
            keys.append(parts[1])
            values.append(parts[2])
        insides = [
            jnp.exp(jnp.where(below, decay_sum[:, h : h + 1] - decay_rows[h : h + 1, :], -1e30))
            for h in everyone
        ]
        key_lows = [keys[h][0].astype(BF) for h in everyone]
        query_lows = [(queries[h][0] * SCALE).astype(BF) for h in everyone]
        dots = [
            mm_nt(jnp.concatenate([key_lows[h], query_lows[h]], axis=0), key_lows[h])
            for h in everyone
        ]
        updates = [upd_ref[0, m, :, own_lanes[h]] for h in everyone]
        states = [st_ref[0, m, h] for h in everyone]
        d_states = [dstate_ref[m, h] for h in everyone]
        d_state_lows = [item.astype(BF) for item in d_states]
        outs = [dots[h][rows:] * insides[h] for h in everyone]
        d_updates = [
            mm_tn(outs[h], d_cores[h]) + mm(keys[h][0] * t_cols[h], d_state_lows[h])
            for h in everyone
        ]
        d_rests = [mm_tn(inv_ref[0, m, h], d_updates[h]) for h in everyone]
        pairs = [
            jnp.concatenate([d_cores[h], d_rests[h].astype(BF)], axis=0) for h in everyone
        ]
        boths = [mm_nt(pairs[h], updates[h]) for h in everyone]
        sides = [mm_nt(pairs[h], states[h]) for h in everyone]
        d_tail_keys = [mm_nt(updates[h], d_state_lows[h]) for h in everyone]
        for h in everyone:
            key, query = keys[h][0], queries[h][0]
            d_weights, d_power = boths[h][:rows], -boths[h][rows:]
            core_state, rest_state = sides[h][:rows], sides[h][rows:]
            key_dots = dots[h][:rows]
            d_query_dots = d_weights * insides[h]
            power_in = jnp.where(strict, d_power * insides[h], 0.0)
            d_key_dots = power_in * b_cols[h][:, :rows]
            reach = d_weights * outs[h] + d_key_dots * key_dots
            key_rest = jnp.sum(key * rest_state, axis=-1, keepdims=True)
            d_beta_col = (
                jnp.sum(power_in * key_dots, axis=-1, keepdims=True)
                + jnp.sum(d_rests[h] * values[h][0], axis=-1, keepdims=True)
                - growth[:, h : h + 1] * key_rest
            )
            d_growth = SCALE * jnp.sum(query * core_state, axis=-1, keepdims=True) - beta[:, heads + h : heads + h + 1] * key_rest
            tail_part = tail[:, h : h + 1] * jnp.sum(d_tail_keys[h] * key, axis=-1, keepdims=True)
            last_part = jnp.sum(tail_part, axis=0, keepdims=True) + keeps[h] * jnp.sum(
                jnp.sum(d_states[h] * states[h].astype(F32), axis=0, keepdims=True),
                axis=-1,
                keepdims=True,
            )
            d_sum_col = (
                jnp.sum(reach, axis=-1, keepdims=True)
                + growth[:, h : h + 1] * d_growth
                - tail_part
                + jnp.where(last_row, last_part, 0.0)
            )
            d_decay = jnp.where(lane_ids == h, d_sum_col, d_decay)
            d_beta = jnp.where(lane_ids == heads + h, d_beta_col, d_beta)
            d_decay_lines = jnp.where(
                line_ids == h, jnp.sum(reach, axis=0, keepdims=True), d_decay_lines
            )
            scale_rest = -(b_cols[h] * g_cols[h])
            dot_grads = jnp.concatenate([d_key_dots, d_query_dots], axis=0).astype(BF)
            by_key = mm(dot_grads, key_lows[h])
            d_query = (g_cols[h] * core_state + by_key[rows:]) * SCALE
            d_key = (
                scale_rest * rest_state
                + t_cols[h] * d_tail_keys[h]
                + by_key[:rows]
                + mm_tn(dot_grads, jnp.concatenate([key_lows[h], query_lows[h]], axis=0))
            )
            dstate_ref[m, h] = keeps[h] * d_states[h] + mm_tn(
                jnp.concatenate([query * (SCALE * g_cols[h]), key * scale_rest], axis=0), pairs[h]
            )
            conv_back(
                m, 0, h, later, queries[h][2],
                queries[h][1] * (d_query - query * jnp.sum(query * d_query, axis=-1, keepdims=True)),
            )
            conv_back(
                m, 1, h, later, keys[h][2],
                keys[h][1] * (d_key - key * jnp.sum(key * d_key, axis=-1, keepdims=True)),
            )
            conv_back(m, 2, h, later, values[h][2], b_cols[h] * d_rests[h] * values[h][1])
        d_log = mm_exact(upper, d_decay - d_decay_lines.T)
        d_arg = d_log * scal_ref[0:1, :] * sigmoid(small + scal_ref[1:2, :])
        dscal_ref[0:1, :] += jnp.sum(d_log * log_alpha, axis=0, keepdims=True)
        dscal_ref[1:2, :] += jnp.sum(d_arg, axis=0, keepdims=True)
        draw_ref[0, m, :, 4 * width : 4 * width + LANES] = (
            d_arg + d_beta * beta * (1.0 - beta)
        ).astype(BF)


def mixer_shapes(raw):
    blocks, group, rows, total = raw.shape
    heads = (total - LANES) // (4 * HD)
    return blocks, group, rows, heads, heads * HD, total


def whole(shape):
    return pl.BlockSpec(shape, lambda c, place: (0,) * len(shape))


PARAMS = dict(dimension_semantics=("arbitrary",), vmem_limit_bytes=56 * 1024 * 1024)


def mixer_forward(place, raw, aux, segrow, conv_rows, scal, gain):
    blocks, group, rows, heads, width, total = mixer_shapes(raw)
    at = lambda c, place: (place[c], 0, 0, 0)
    seq = lambda c, place: (c, 0, 0, 0)
    seq5 = lambda c, place: (c, 0, 0, 0, 0)
    fact = lambda c, place: (0, c, 0, 0)

    def body(*refs):
        forward_kernel(heads, *refs)

    return pl.pallas_call(
        body,
        grid_spec=pltpu.PrefetchScalarGridSpec(
            num_scalar_prefetch=1,
            grid=(blocks,),
            in_specs=[
                pl.BlockSpec((1, group, rows, total), at),
                pl.BlockSpec((group, 1, rows, 16), fact),
                pl.BlockSpec((group, 1, 8, rows), fact),
                whole(conv_rows.shape),
                whole(scal.shape),
                whole(gain.shape),
            ],
            out_specs=[
                pl.BlockSpec((1, group, rows, width), at),
                pl.BlockSpec((1, group, rows, width), seq),
                pl.BlockSpec((1, group, heads, rows, rows), seq5),
                pl.BlockSpec((1, group, rows, width), seq),
                pl.BlockSpec((1, group, heads, HD, HD), seq5),
            ],
            scratch_shapes=[
                pltpu.VMEM((group, rows + 8, 3 * width), F32),
                pltpu.VMEM((group, heads, HD, HD), F32),
            ],
        ),
        out_shape=[
            jax.ShapeDtypeStruct((blocks, group, rows, width), BF),
            jax.ShapeDtypeStruct((blocks, group, rows, width), F32),
            jax.ShapeDtypeStruct((blocks, group, heads, rows, rows), BF),
            jax.ShapeDtypeStruct((blocks, group, rows, width), BF),
            jax.ShapeDtypeStruct((blocks, group, heads, HD, HD), BF),
        ],
        compiler_params=pltpu.CompilerParams(**PARAMS),
        cost_estimate=pl.CostEstimate(
            flops=FORWARD_COST * blocks * group * heads, bytes_accessed=8_000_000, transcendentals=0
        ),
        name="mixer_forward",
    )(place, raw, aux, segrow, conv_rows, scal, gain)


def mixer_backward(place, raw, aux, segrow, conv_rows, scal, gain, d_mixed, saved):
    blocks, group, rows, heads, width, total = mixer_shapes(raw)
    core, inverse, update, states = saved
    back = lambda c: blocks - 1 - c
    at = lambda c, place: (place[back(c)], 0, 0, 0)
    before = lambda c, place: (place[jnp.maximum(back(c) - 1, 0)], 0, rows // 8 - 1, 0)
    seq = lambda c, place: (back(c), 0, 0, 0)
    seq5 = lambda c, place: (back(c), 0, 0, 0, 0)
    fact = lambda c, place: (0, back(c), 0, 0)

    def body(*refs):
        backward_kernel(heads, *refs)

    return pl.pallas_call(
        body,
        grid_spec=pltpu.PrefetchScalarGridSpec(
            num_scalar_prefetch=1,
            grid=(blocks,),
            in_specs=[
                pl.BlockSpec((1, group, rows, total), at),
                pl.BlockSpec((1, group, 8, total), before),
                pl.BlockSpec((group, 1, rows, 16), fact),
                pl.BlockSpec((group, 1, 8, rows), fact),
                whole(conv_rows.shape),
                whole(scal.shape),
                whole(gain.shape),
                pl.BlockSpec((1, group, rows, width), at),
                pl.BlockSpec((1, group, rows, width), seq),
                pl.BlockSpec((1, group, heads, rows, rows), seq5),
                pl.BlockSpec((1, group, rows, width), seq),
                pl.BlockSpec((1, group, heads, HD, HD), seq5),
            ],
            out_specs=[
                pl.BlockSpec((1, group, rows, total), at),
                whole((96, width)),
                whole((8, LANES)),
                whole((8, width)),
            ],
            scratch_shapes=[
                pltpu.VMEM((group, rows + 8, 3 * width), F32),
                pltpu.VMEM((group, rows + 8, 3 * width), F32),
                pltpu.VMEM((group, heads, HD, HD), F32),
            ],
        ),
        out_shape=[
            jax.ShapeDtypeStruct((blocks, group, rows, total), BF),
            jax.ShapeDtypeStruct((96, width), F32),
            jax.ShapeDtypeStruct((8, LANES), F32),
            jax.ShapeDtypeStruct((8, width), F32),
        ],
        compiler_params=pltpu.CompilerParams(**PARAMS),
        cost_estimate=pl.CostEstimate(
            flops=BACKWARD_COST * blocks * group * heads, bytes_accessed=12_000_000, transcendentals=0
        ),
        name="mixer_backward",
    )(place, raw, raw, aux, segrow, conv_rows, scal, gain, d_mixed, core, inverse, update, states)


def hop(values, bit, axis="head"):
    size = lax.axis_size(axis)
    return lax.ppermute(values, axis, [(i, i ^ bit) for i in range(size)])


def after(values, *earlier):
    kept = [item for group in earlier for item in (group if isinstance(group, list) else [group])]
    if not kept:
        return values
    return lax.optimization_barrier((values, *kept))[0]


def butterfly(values, axes):
    for axis in axes:
        bit = 1
        while bit < lax.axis_size(axis):
            values = values + hop(values, bit, axis)
            bit *= 2
    return values


def gather_near(values, *earlier):
    if earlier:
        values = after(values, *earlier)
    if lax.axis_size("head") != 4:
        return [lax.all_gather(values, "head", axis=0, tiled=True)]
    return [values, hop(values, 1), hop(values, 2)]


def gather_far(near, *earlier):
    if len(near) == 1:
        return []
    half = near[0].shape[0] // 2
    from_x, from_y = after(near[1], *earlier), after(near[2], *earlier)
    return [hop(from_y[:half], 1), hop(from_x[half:], 2)]


def block_parts(size, rows):
    if size != 4:
        return [[(0, r * rows, rows)] for r in range(size)]
    half = rows // 2
    return [[(0, 0, rows)], [(1, 0, rows)], [(2, 0, rows)], [(3, 0, half), (4, 0, half)]]


def joined(arrays):
    return arrays[0] if len(arrays) == 1 else jnp.concatenate(arrays, axis=0)


def scatter_plan(size, rows):
    half = rows // 2
    if size != 4:
        return [size * rows], {(r, h): (0, r * rows + h * half) for r in range(size) for h in (0, 1)}
    return [rows, rows, 2 * rows], {
        (1, 0): (0, 0), (3, 0): (0, half),
        (2, 1): (1, 0), (3, 1): (1, half),
        (0, 0): (2, 0), (0, 1): (2, half), (2, 0): (2, 2 * half), (1, 1): (2, 3 * half),
    }


def scatter_near(arrays, *earlier):
    if len(arrays) == 1:
        part = after(arrays[0], *earlier)
        return [lax.psum_scatter(part, "head", scatter_dimension=0, tiled=True)]
    to_x, to_y, keep = arrays
    return [hop(after(to_x, *earlier), 1), hop(after(to_y, *earlier), 2), keep]


def scatter_far(near, *earlier, before_end=()):
    if len(near) == 1:
        return near[0].astype(F32)
    in_x, in_y, keep = [after(item, *earlier) for item in near]
    half = in_x.shape[0] // 2
    pass_y = (keep[2 * half : 3 * half].astype(F32) + in_x[half:].astype(F32)).astype(BF)
    pass_x = (keep[3 * half :].astype(F32) + in_y[half:].astype(F32)).astype(BF)
    last_y = after(hop(pass_y, 2), *before_end).astype(F32)
    last_x = after(hop(pass_x, 1), *before_end).astype(F32)
    near_sum = jnp.concatenate([in_x[:half], in_y[:half]], axis=0).astype(F32)
    last = jnp.concatenate([last_y, last_x], axis=0)
    return keep[: 2 * half].astype(F32) + near_sum + last


def scatter_kernel(size, where, transposed, x_ref, w_ref, *refs):
    outs, buf, sem = refs[:-2], refs[-2], refs[-1]
    step = pl.program_id(0)
    half = x_ref.shape[0] // 2
    slot = lax.rem(step, 2)

    def stores(block):
        return [
            pltpu.make_async_copy(
                buf.at[block % 2, h * half : (h + 1) * half],
                outs[where[(block, h)][0]].at[where[(block, h)][1] : where[(block, h)][1] + half],
                sem.at[block % 2, h],
            )
            for h in (0, 1)
        ]

    for block in range(2, size):
        @pl.when(step == block)
        def _(block=block):
            for copy in stores(block - 2):
                copy.wait()

    x = x_ref[...]
    buf[slot] = (mm_nt(x, w_ref[...]) if transposed else mm(x, w_ref[...])).astype(BF)
    for block in range(size):
        @pl.when(step == block)
        def _(block=block):
            for copy in stores(block):
                copy.start()
            if block == size - 1:
                for earlier in range(max(0, size - 2), size):
                    for copy in stores(earlier):
                        copy.wait()


def scatter_matmul(values, weight, size, transposed=False):
    rows = values.shape[0] // size
    width = weight.shape[0] if transposed else weight.shape[1]
    counts, where = scatter_plan(size, rows)
    return list(pl.pallas_call(
        lambda *refs: scatter_kernel(size, where, transposed, *refs),
        grid=(size,),
        in_specs=[
            pl.BlockSpec((rows, values.shape[1]), lambda i: (i, 0)),
            pl.BlockSpec(weight.shape, lambda i: (0, 0)),
        ],
        out_specs=[pl.BlockSpec(memory_space=pl.ANY)] * len(counts),
        out_shape=[jax.ShapeDtypeStruct((count, width), BF) for count in counts],
        scratch_shapes=[pltpu.VMEM((2, rows, width), BF), pltpu.SemaphoreType.DMA((2, 2))],
        compiler_params=pltpu.CompilerParams(**PARAMS),
        cost_estimate=pl.CostEstimate(
            flops=4 * values.size * width, bytes_accessed=15_000_000, transcendentals=0
        ),
        name="scatter_matmul",
    )(values, weight))


def ffn_kernel(turns, rows, parts, n_pieces, where, n_out, aliased, *refs):
    mids, cots = refs[:n_pieces], refs[n_pieces : 2 * n_pieces]
    wg_ref, wu_ref, wd_ref = refs[2 * n_pieces : 2 * n_pieces + 3]
    refs = refs[2 * n_pieces + 3 + (2 * n_out if aliased else 0) :]
    act_ref, dg_ref, du_ref, xo_ref, co_ref = refs[:5]
    gm_refs, ff_refs = refs[5 : 5 + n_out], refs[5 + n_out : 5 + 2 * n_out]
    wg, wu, wd, xbuf, cbuf, gm_buf, ff_buf, w_sem, x_sem, c_sem, o_sem = refs[5 + 2 * n_out :]
    step = pl.program_id(0)
    half = rows // 2
    steps = len(turns)

    def loads(turn):
        slot = turn % 2
        found = []
        for arrays, buf, sem in ((mids, xbuf, x_sem), (cots, cbuf, c_sem)):
            place = 0
            for k, (index, at, count) in enumerate(parts[turns[turn]]):
                found.append(
                    pltpu.make_async_copy(
                        arrays[index].at[at : at + count],
                        buf.at[slot, place : place + count],
                        sem.at[slot, k],
                    )
                )
                place += count
        return found

    def stores(turn):
        slot = turn % 2
        found = []
        for k, (buf, outs) in enumerate(((gm_buf, gm_refs), (ff_buf, ff_refs))):
            for h in (0, 1):
                index, at = where[(turns[turn], h)]
                found.append(
                    pltpu.make_async_copy(
                        buf.at[slot, h * half : (h + 1) * half],
                        outs[index].at[at : at + half],
                        o_sem.at[slot, 2 * k + h],
                    )
                )
        return found

    weights = [
        pltpu.make_async_copy(src, dst, w_sem.at[k])
        for k, (src, dst) in enumerate(((wg_ref, wg), (wu_ref, wu), (wd_ref, wd)))
    ]

    @pl.when(step == 0)
    def _():
        for copy in loads(0):
            copy.start()
        for copy in weights:
            copy.start()

    for turn in range(steps):
        @pl.when(step == turn)
        def _(turn=turn):
            if turn + 1 < steps:
                for copy in loads(turn + 1):
                    copy.start()
            for copy in loads(turn):
                copy.wait()
            if turn >= 2:
                for copy in stores(turn - 2):
                    copy.wait()

    slot = lax.rem(step, 2)

    @pl.when(step == 0)
    def _():
        weights[0].wait()

    x = xbuf[slot]
    gate = jnp.dot(x, wg[...], preferred_element_type=F32)

    @pl.when(step == 0)
    def _():
        weights[1].wait()

    upward = jnp.dot(x, wu[...], preferred_element_type=F32)

    @pl.when(step == 0)
    def _():
        weights[2].wait()

    cot = cbuf[slot]
    d_act = jnp.dot(cot, wd[...], preferred_element_type=F32)
    open_ = sigmoid(gate)
    silu = gate * open_
    act = (silu * upward).astype(BF)
    d_gate = (d_act * upward * open_ * (1.0 + gate * (1.0 - open_))).astype(BF)
    d_up = (d_act * silu).astype(BF)
    act_ref[0] = act
    dg_ref[0] = d_gate
    du_ref[0] = d_up
    xo_ref[0] = x
    co_ref[0] = cot
    gm_buf[slot] = (mm_nt(d_gate, wg[...]) + mm_nt(d_up, wu[...])).astype(BF)
    ff_buf[slot] = mm_nt(act, wd[...]).astype(BF)
    for turn in range(steps):
        @pl.when(step == turn)
        def _(turn=turn):
            for copy in stores(turn):
                copy.start()
            if turn == steps - 1:
                for earlier in range(max(0, steps - 2), steps):
                    for copy in stores(earlier):
                        copy.wait()


def ffn_stage(turns, mids, cots, weights, size, filled=None):
    width, hidden = weights[0].shape
    rows = mids[0].shape[0] if size == 4 else mids[0].shape[0] // size
    parts = block_parts(size, rows)
    counts, where = scatter_plan(size, rows)
    aliased = filled is not None
    filled = list(filled) if aliased else []

    def body(*refs):
        ffn_kernel(turns, rows, parts, len(mids), where, len(counts), aliased, *refs)

    anywhere = pl.BlockSpec(memory_space=pl.ANY)
    by_block = lambda last: pl.BlockSpec((1, rows, last), lambda i: (i, 0, 0))
    steps = len(turns)
    first = 2 * len(mids) + 3
    out = pl.pallas_call(
        body,
        grid=(steps,),
        in_specs=[anywhere] * (first + len(filled)),
        out_specs=[by_block(hidden)] * 3 + [by_block(width)] * 2 + [anywhere] * (2 * len(counts)),
        out_shape=[jax.ShapeDtypeStruct((steps, rows, hidden), BF)] * 3
        + [jax.ShapeDtypeStruct((steps, rows, width), BF)] * 2
        + [jax.ShapeDtypeStruct((c, width), BF) for c in counts] * 2,
        input_output_aliases={first + k: 5 + k for k in range(len(filled))},
        scratch_shapes=[
            pltpu.VMEM((width, hidden), BF),
            pltpu.VMEM((width, hidden), BF),
            pltpu.VMEM((width, hidden), BF),
            pltpu.VMEM((2, rows, width), BF),
            pltpu.VMEM((2, rows, width), BF),
            pltpu.VMEM((2, rows, width), BF),
            pltpu.VMEM((2, rows, width), BF),
            pltpu.SemaphoreType.DMA((3,)),
            pltpu.SemaphoreType.DMA((2, 2)),
            pltpu.SemaphoreType.DMA((2, 2)),
            pltpu.SemaphoreType.DMA((2, 4)),
        ],
        compiler_params=pltpu.CompilerParams(**PARAMS),
        cost_estimate=pl.CostEstimate(
            flops=steps * rows * width * hidden * 20, bytes_accessed=30_000_000, transcendentals=0
        ),
        name="ffn_stage",
    )(*mids, *cots, *weights, *filled)
    flat = [array.reshape(steps * rows, array.shape[-1]) for array in out[:5]]
    return flat, list(out[5:])


def piece_kernel(size, parts, n_pieces, transposed, *refs):
    pieces, w_ref, out_ref, copy_ref, xbuf, x_sem = refs[:n_pieces], *refs[n_pieces:]
    step = pl.program_id(0)

    def loads(block):
        slot = block % 2
        found, place = [], 0
        for k, (index, at, count) in enumerate(parts[block]):
            found.append(
                pltpu.make_async_copy(
                    pieces[index].at[at : at + count],
                    xbuf.at[slot, place : place + count],
                    x_sem.at[slot, k],
                )
            )
            place += count
        return found

    for block in range(size):
        @pl.when(step == block)
        def _(block=block):
            if block == 0:
                for copy in loads(0):
                    copy.start()
            if block + 1 < size:
                for copy in loads(block + 1):
                    copy.start()
            for copy in loads(block):
                copy.wait()

    x = xbuf[lax.rem(step, 2)]
    copy_ref[0] = x
    out_ref[0] = mm_nt(x, w_ref[...]) if transposed else mm(x, w_ref[...])


def piece_matmul(pieces, weight, size, transposed=False):
    width = pieces[0].shape[1]
    rows = pieces[0].shape[0] if size == 4 else pieces[0].shape[0] // size
    columns = weight.shape[0] if transposed else weight.shape[1]
    parts = block_parts(size, rows)
    return pl.pallas_call(
        lambda *refs: piece_kernel(size, parts, len(pieces), transposed, *refs),
        grid=(size,),
        in_specs=[pl.BlockSpec(memory_space=pl.ANY)] * len(pieces)
        + [pl.BlockSpec(weight.shape, lambda i: (0, 0))],
        out_specs=[
            pl.BlockSpec((1, rows, columns), lambda i: (i, 0, 0)),
            pl.BlockSpec((1, rows, width), lambda i: (i, 0, 0)),
        ],
        out_shape=[
            jax.ShapeDtypeStruct((size, rows, columns), F32),
            jax.ShapeDtypeStruct((size, rows, width), BF),
        ],
        scratch_shapes=[pltpu.VMEM((2, rows, width), BF), pltpu.SemaphoreType.DMA((2, 2))],
        compiler_params=pltpu.CompilerParams(**PARAMS),
        cost_estimate=pl.CostEstimate(
            flops=4 * size * rows * width * columns, bytes_accessed=30_000_000, transcendentals=0
        ),
        name="piece_matmul",
    )(*pieces, weight)


def wgrad_kernel(count, *refs):
    lefts, rights, rest = refs[:count], refs[count : 2 * count], refs[2 * count :]
    total = mm_tn(lefts[0][...], rights[0][...])
    for left, right in zip(lefts[1:], rights[1:]):
        total = total + mm_tn(left[...], right[...])
    out_ref = rest[-1]
    if len(rest) == 1:
        out_ref[...] = total.astype(BF)
    else:
        columns = total.shape[1]
        out_ref[:, :columns] = total.astype(BF)
        out_ref[:, columns:] = rest[0][...]


def weight_gradient(lefts, rights, beside=None):
    wide = lefts[0].shape[1]
    columns = rights[0].shape[1]
    extra = [] if beside is None else [beside]
    full = columns + sum(item.shape[1] for item in extra)
    tile = 512 if wide % 512 == 0 else wide
    count = len(lefts)
    depth = sum(left.shape[0] for left in lefts)
    return pl.pallas_call(
        lambda *refs: wgrad_kernel(count, *refs),
        grid=(wide // tile,),
        in_specs=[pl.BlockSpec((left.shape[0], tile), lambda i: (0, i)) for left in lefts]
        + [pl.BlockSpec(right.shape, lambda i: (0, 0)) for right in rights]
        + [pl.BlockSpec((tile, item.shape[1]), lambda i: (i, 0)) for item in extra],
        out_specs=pl.BlockSpec((tile, full), lambda i: (i, 0)),
        out_shape=jax.ShapeDtypeStruct((wide, full), BF),
        compiler_params=pltpu.CompilerParams(**PARAMS),
        cost_estimate=pl.CostEstimate(
            flops=3 * depth * wide * columns, bytes_accessed=20_000_000, transcendentals=0
        ),
        name="weight_gradient",
    )(*lefts, *rights, *extra)


def block_places(size):
    base = lax.iota(jnp.int32, size)
    if size != 4:
        return base
    return base ^ lax.axis_index("head").astype(jnp.int32)


def contract_rows(left, right):
    return lax.dot_general(left, right, (((0,), (0,)), ((), ())), preferred_element_type=F32)


def contract_cols(left, right):
    return lax.dot_general(left, right, (((1,), (1,)), ((), ())), preferred_element_type=F32)


def times(left, right):
    return jnp.dot(left, right, preferred_element_type=F32)


def sequence_facts(doc_lengths, blocks, rows):
    span = blocks * rows
    ends = jnp.cumsum(doc_lengths, axis=-1)
    places = lax.iota(jnp.int32, span)
    segment = jnp.sum((places[None, :, None] >= ends[:, None, :]).astype(jnp.int32), axis=-1)
    columns = [segment]
    for j in range(1, 4):
        columns.append(
            (jnp.pad(segment, ((0, 0), (j, 0)), constant_values=-1)[:, :-j] == segment)
        )
    by_chunk = segment.reshape(-1, blocks, rows)
    prior = jnp.pad(by_chunk[:, :-1, -1], ((0, 0), (1, 0)), constant_values=-1)
    columns.append((by_chunk == prior[:, :, None]).reshape(segment.shape))
    columns.append((by_chunk == by_chunk[:, :, -1:]).reshape(segment.shape))
    columns += [jnp.zeros_like(segment)] * 2
    for j in range(1, 4):
        columns.append(
            (jnp.pad(segment, ((0, 0), (0, j)), constant_values=-1)[:, j:] == segment)
        )
    columns += [jnp.zeros_like(segment)] * (16 - len(columns))
    aux = jnp.stack([item.astype(F32) for item in columns], axis=-1)
    aux = aux.reshape(-1, blocks, rows, 16)
    lines = jnp.broadcast_to(by_chunk.astype(F32)[:, :, None, :], by_chunk.shape[:2] + (8, rows))
    return aux, lines


def on_device(
    tokens, cotangent, token_counts, doc_lengths, norm_in, w_query, w_key, w_value, w_outgate,
    w_decay, w_beta, conv_weight, decay_log, dt_bias, gain_out, w_out, norm_mid, w_gate, w_up,
    w_down,
):
    micro_count, rows, width = tokens.shape
    blocks = lax.axis_size("head")
    group = micro_count // 2
    own_rows = group * rows
    span = own_rows * blocks
    heads = decay_log.shape[0]
    own = heads * HD
    groups = range(micro_count // group)
    my_places = lax.axis_index("head") * rows + lax.iota(jnp.int32, rows)
    live = (my_places[None, :] < token_counts[:, :1]).astype(F32)[:, :, None]
    place = block_places(blocks)
    aux, lines = sequence_facts(doc_lengths[:, 0], blocks, rows)
    conv_rows = jnp.pad(conv_weight.reshape(12, own), ((0, 4), (0, 0)))
    scal = jnp.zeros((8, LANES), F32)
    scal = scal.at[0, :heads].set(-jnp.exp(decay_log)).at[1, :heads].set(dt_bias)
    gain_row = jnp.broadcast_to(gain_out[None], (8, own))
    ffn_gate = lax.all_gather(w_gate, "dp", axis=0, tiled=True)
    ffn_up = lax.all_gather(w_up, "dp", axis=0, tiled=True)
    ffn_down = lax.all_gather(w_down, "dp", axis=0, tiled=True)

    def of_group(array, i):
        return array[i * group : (i + 1) * group]

    inputs, grads, lives, pulls_in, normed_in = [], [], [], [], []
    for i in groups:
        x = of_group(tokens, i).reshape(own_rows, width).astype(F32)
        normed, pull = jax.vjp(norm_rows, x, norm_in)
        inputs.append(x)
        pulls_in.append(pull)
        normed_in.append(normed.astype(BF))
        grads.append((of_group(cotangent, i).astype(F32) * of_group(live, i)).reshape(own_rows, width))
    cots = [item.astype(BF) for item in grads]
    in_a1 = gather_near(normed_in[0])
    w_in = jnp.concatenate(
        [w_query, w_key, w_value, w_outgate, w_decay, w_beta,
         jnp.zeros((width, LANES - 2 * heads), BF)], axis=1
    )

    def project(pieces):
        raw, full = piece_matmul(pieces, w_in, blocks)
        return raw.reshape(blocks, group, rows, 4 * own + LANES), full.reshape(span, width)

    def mix(raw, i):
        mixed, *saved = mixer_forward(
            place, raw, of_group(aux, i), of_group(lines, i), conv_rows, scal, gain_row
        )
        return mixed.reshape(span, own), saved

    def out_of(mixed):
        return scatter_matmul(mixed, w_out, blocks)

    def middle(i, attn):
        resid = inputs[i] + attn
        normed, pull = jax.vjp(norm_rows, resid, norm_mid)
        return resid, pull, normed.astype(BF)

    in_a2 = gather_far(in_a1)
    in_b1 = gather_near(normed_in[1], in_a2)
    raw_a, full_a = project(in_a1 + in_a2)
    in_b2 = gather_far(in_b1, raw_a)
    cot_a1 = gather_near(cots[0], in_b1)
    mixed_a, saved_a = mix(after(raw_a, in_b1), 0)
    attn_a = out_of(after(mixed_a, in_b2))
    at_a1 = scatter_near(attn_a)
    pieces_b = in_b1 + in_b2
    raw_b, full_b = project([after(pieces_b[0], attn_a, cot_a1)] + pieces_b[1:])
    sum_a = scatter_far(at_a1, raw_b)
    cot_a2 = gather_far(cot_a1, raw_b)
    mixed_b, saved_b = mix(after(raw_b, at_a1), 1)
    resid_a, pull_a, mid_a = middle(0, sum_a)
    mid_a1 = gather_near(mid_a)
    attn_b = out_of(after(mixed_b, mid_a, cot_a2))
    at_b1 = scatter_near(attn_b, mid_a1)
    mid_a2 = gather_far(mid_a1, attn_b)

    ffn_weights = [ffn_gate, ffn_up, ffn_down]
    first_turns = (1, 3) if blocks == 4 else tuple(range(blocks // 2))
    last_turns = tuple(r for r in range(blocks) if r not in first_turns)
    outs = len(scatter_plan(blocks, own_rows)[0])
    near_a = mid_a1 + mid_a2
    near_a[0] = after(near_a[0], at_b1)
    sum_b = scatter_far(at_b1, mid_a2)
    cot_b1 = gather_near(cots[1], at_b1, mid_a2)
    kept_a, begun = ffn_stage(first_turns, near_a, cot_a1 + cot_a2, ffn_weights, blocks)
    resid_b, pull_b, mid_b = middle(1, sum_b)
    mid_b1 = gather_near(mid_b)
    cot_b2 = gather_far(cot_b1, kept_a[0])
    begun[0] = after(begun[0], mid_b1, cot_b1)
    kept_a2, out_a = ffn_stage(
        last_turns, near_a, cot_a1 + cot_a2, ffn_weights, blocks, begun
    )
    mid_b2 = gather_far(mid_b1, kept_a[0])
    gm_a1 = scatter_near(out_a[:outs], mid_b2, cot_b2)
    near_b = mid_b1 + mid_b2
    near_b[0] = after(near_b[0], out_a[0])
    kept_b, begun = ffn_stage(first_turns, near_b, cot_b1 + cot_b2, ffn_weights, blocks)
    d_mid_a = scatter_far(gm_a1, kept_b[0])
    begun = [after(begun[0], gm_a1)] + begun[1:]
    kept_b2, out_b = ffn_stage(last_turns, near_b, cot_b1 + cot_b2, ffn_weights, blocks, begun)
    kept = [kept_a, kept_a2, kept_b, kept_b2]
    acts, gates, ups, mids, cot_all = [[item[k] for item in kept] for k in range(5)]

    def share(term):
        return lax.psum_scatter(term, "dp", scatter_dimension=0, tiled=True).astype(F32)

    def resid_back(i, pull, d_mid):
        d_resid, d_norm = pull(d_mid)
        d_resid = grads[i] + d_resid
        return d_resid, d_norm, d_resid.astype(BF)

    gm_b1 = scatter_near(out_b[:outs], d_mid_a)
    d_resid_a, gain_mid_a, low_a = resid_back(0, pull_a, d_mid_a)
    rg_a1 = gather_near(low_a)
    gates[0] = after(gates[0], low_a)
    term_gate = weight_gradient(mids, gates)
    grad_gate = share(term_gate)
    ups[0] = after(ups[0], term_gate)
    term_up = weight_gradient(mids, ups)
    grad_up = share(after(term_up, rg_a1, gm_b1))
    rg_a2 = gather_far(rg_a1, term_up)
    d_mid_b = scatter_far(gm_b1, term_up)
    acts[0] = after(acts[0], term_up, rg_a1, gm_b1)
    term_down = weight_gradient(cot_all, acts)
    d_resid_b, gain_mid_b, low_b = resid_back(1, pull_b, after(d_mid_b, term_down, rg_a2))
    grad_down = share(after(term_down, low_b))
    rg_b1 = gather_near(low_b)
    ff_a1 = scatter_near(out_a[outs:], low_b)

    def to_mixed(pieces):
        d_mixed, full = piece_matmul(pieces, w_out, blocks, transposed=True)
        return d_mixed.reshape(blocks, group, rows, own), full.reshape(span, width)

    def mix_back(i, d_mixed, raw, saved):
        d_raw, *sums = mixer_backward(
            place, raw, of_group(aux, i), of_group(lines, i), conv_rows, scal, gain_row,
            d_mixed, saved,
        )
        return d_raw.reshape(span, 4 * own + LANES), sums

    def in_back(d_raw):
        return scatter_matmul(d_raw, w_in, blocks, transposed=True)

    pieces_ra = rg_a1 + rg_a2
    pieces_ra[0] = after(pieces_ra[0], low_b)
    d_mixed_a, full_ra = to_mixed(pieces_ra)
    d_raw_a, sums_a = mix_back(0, d_mixed_a, raw_a, saved_a)
    rg_b2 = gather_far(rg_b1, d_raw_a)
    ffn_a = scatter_far(ff_a1, d_raw_a)
    d_in_a = in_back(after(d_raw_a, ff_a1, rg_b1))
    gi_a1 = scatter_near(d_in_a)
    pieces_rb = rg_b1 + rg_b2
    pieces_rb[0] = after(pieces_rb[0], d_in_a, ffn_a)
    d_mixed_b, full_rb = to_mixed(pieces_rb)
    term_out = weight_gradient([full_ra, full_rb], [after(mixed_a, d_mixed_b), mixed_b])
    grad_out = share(term_out).T
    ff_b1 = scatter_near(out_b[outs:], gi_a1)
    d_raw_b, sums_b = mix_back(1, after(d_mixed_b, term_out, gi_a1), raw_b, saved_b)
    term_in = weight_gradient([full_a, full_b], [d_raw_a, after(d_raw_b, ff_b1, grad_gate, grad_up)])
    grad_in = share(term_in)
    d_in_b = in_back(after(d_raw_b, term_in, grad_down))
    d_norm_a = scatter_far(gi_a1, term_out, before_end=[d_raw_b])
    ffn_b = scatter_far(ff_b1, d_raw_b, before_end=d_in_b[:1])
    gi_b1 = scatter_near(d_in_b)
    d_norm_b = scatter_far(gi_b1)

    results, input_grads = [], []
    gain_in = jnp.zeros_like(norm_in)
    for i, (resid, ffn, d_resid, d_norm) in enumerate(
        ((resid_a, ffn_a, d_resid_a, d_norm_a), (resid_b, ffn_b, d_resid_b, d_norm_b))
    ):
        results.append((resid + ffn).astype(BF).reshape(group, rows, width))
        d_inputs, d_gain = pulls_in[i](d_norm)
        input_grads.append((d_inputs + d_resid).astype(BF).reshape(group, rows, width))
        gain_in = gain_in + d_gain
    gain_mid = gain_mid_a + gain_mid_b
    small_sums = [left + right for left, right in zip(sums_a, sums_b)]
    conv_sum = jnp.sum(small_sums[0].reshape(12, 8, own), axis=1)
    scal_sum = jnp.pad(small_sums[1][:2, :heads], ((0, 0), (0, own - heads)))
    wide = jnp.concatenate([conv_sum, small_sums[2][:1], scal_sum, jnp.zeros((1, own), F32)], axis=0)
    wide = butterfly(after(wide, term_in), ("dp",))
    narrow = wide[13:15]
    gains = butterfly(jnp.stack([gain_in, gain_mid]), ("dp", "head"))
    return (
        jnp.concatenate(results, axis=0),
        jnp.concatenate(input_grads, axis=0),
        gains[0],
        grad_in[:, :own],
        grad_in[:, own : 2 * own],
        grad_in[:, 2 * own : 3 * own],
        grad_in[:, 3 * own : 4 * own],
        grad_in[:, 4 * own : 4 * own + heads],
        grad_in[:, 4 * own + heads : 4 * own + 2 * heads],
        wide[:12].reshape(conv_weight.shape),
        narrow[0, :heads],
        narrow[1, :heads],
        wide[12],
        grad_out,
        gains[1],
        grad_gate,
        grad_up,
        grad_down,
    )


def solution(mesh):
    return jax.shard_map(
        on_device,
        mesh=mesh,
        in_specs=(
            P(None, ("dp", "head"), None),
            P(None, ("dp", "head"), None),
            P(None, "dp"),
            P(None, "dp", None),
            P(),
            P(None, "head"),
            P(None, "head"),
            P(None, "head"),
            P(None, "head"),
            P(None, "head"),
            P(None, "head"),
            P(None, None, "head"),
            P("head"),
            P("head"),
            P("head"),
            P("head", None),
            P(),
            P("dp", "head"),
            P("dp", "head"),
            P("dp", "head"),
        ),
        out_specs=(
            P(None, ("dp", "head"), None),
            P(None, ("dp", "head"), None),
            P(),
            P("dp", "head"),
            P("dp", "head"),
            P("dp", "head"),
            P("dp", "head"),
            P("dp", "head"),
            P("dp", "head"),
            P(None, None, "head"),
            P("head"),
            P("head"),
            P("head"),
            P("head", "dp"),
            P(),
            P("dp", "head"),
            P("dp", "head"),
            P("dp", "head"),
        ),
        check_vma=False,
    )
```
